128 devices in a mesh: fx: 8 (over z, core), fy: 16 (over x, y).
Axes of the slice: x: 4, y: 4, z: 4, core: 2. Of those that a mesh axis runs over, the one named last changes fastest.
Arguments:
- tracers: float32 [8, 72, 128, 2048], P(None, None, 'fx', 'fy'), may hold values from -6 to 6
- group_dest: int32 [128, 2048], P('fx', 'fy'), may hold values from 0 to 127, as said below
- group_slot: int32 [128, 2048], P('fx', 'fy'), may hold values from 0 to 2047, as said below
- diffusivity: float32 [72, 262144], P(None, ('fx', 'fy')), may hold values from 0.05 to 5
- surface_flux: float32 [8, 262144], P(None, ('fx', 'fy')), may hold values from -6 to 6
Outputs:
- tracers_out: float32 [8, 72, 128, 2048], P(None, None, 'fx', 'fy')
The draws below stay inside these ranges and needn't reach their ends.
Inputs may be any that keep to these rules, and one draw needn't show every extreme that they name: `group_dest`: on every device exactly 512 columns name another device and every device is named by exactly 512 columns of other devices; at most 6 columns of one device name one other device, exactly 6 for some pairs; the number of columns of device r that name device (r + o) mod 128 depends on o only. `group_slot`: together with group_dest it names every physics slot of all devices exactly once.
All inputs are finite; a program needn't handle non-finite values.
Results may differ from the reference program's by a relative error of at most 0.00002.
Values sent between devices are 32-bit elements; how exact they have to be, the bound alone decides.
A program may use at most 128 MiB of HBM per device.

```python
import math
import jax
import jax.numpy as jnp
from jax import lax

TRACERS = 8
LEV = 72
CX = 16
CY = 128
COLS = 2048
MOVED = 512
CAP = 6
NX = 128
NY = 2048
NCHUNK = 262144
N_FX = 8
N_FY = 16
DEVICES = 128


def to_grid(table):
    return table.reshape(N_FX, N_FY, CX, CY).transpose(0, 2, 1, 3).reshape(N_FX * CX, N_FY * CY)


def group_tables(key):
    order_key, slot_key, offset_key = jax.random.split(key, 3)

    def shuffle(subkey):
        return jax.random.permutation(subkey, COLS).astype(jnp.int32)
    source_order = jax.vmap(shuffle)(jax.random.split(order_key, DEVICES))
    slot_order = jax.vmap(shuffle)(jax.random.split(slot_key, DEVICES))
    scores = jax.random.permutation(offset_key, DEVICES - 1).astype(jnp.int32) + 3
    first_ones = jnp.array([DEVICES // 2 - 1, 0, DEVICES - 2], dtype=jnp.int32)
    scores = scores.at[first_ones].set(jnp.array([0, 1, 2], dtype=jnp.int32))
    offsets = jnp.argsort(scores, stable=True).astype(jnp.int32) + 1
    rank_index = jnp.arange(COLS, dtype=jnp.int32)
    others = jnp.maximum(rank_index - CAP, 0) % (DEVICES - 2)
    offset = jnp.where(rank_index < CAP, offsets[0], offsets[1 + others])
    device_grid = jnp.broadcast_to(jnp.arange(DEVICES, dtype=jnp.int32)[:, None], (DEVICES, COLS))
    moving = rank_index[None, :] < MOVED
    target = jnp.where(moving, (device_grid + offset[None, :]) % DEVICES, device_grid)
    rank_grid = jnp.broadcast_to(rank_index[None, :], (DEVICES, COLS))
    group_slots = slot_order[target, rank_grid]
    dest_table = jnp.zeros((DEVICES, COLS), jnp.int32).at[device_grid, source_order].set(target)
    slot_table = jnp.zeros((DEVICES, COLS), jnp.int32).at[device_grid, source_order].set(group_slots)
    return (to_grid(dest_table), to_grid(slot_table))


def draw_group_dest(key, part):
    return group_tables(key)[0]


def draw_group_slot(key, part):
    return group_tables(key)[1]


def block_levels(rng, dims, pieces, smallest, top_value):
    def one(axis_at, parts):
        steps = jax.random.uniform(jax.random.fold_in(jax.random.fold_in(rng, 6), axis_at), (parts,), jnp.float32, smallest / len(pieces), top_value / len(pieces))
        return jnp.repeat(jnp.exp(steps), dims[axis_at] // parts).reshape((-1,) + (1,) * (len(dims) - axis_at - 1))

    factor_of = one(*pieces[0])
    for cut in pieces[1:]:
        factor_of = factor_of * one(*cut)
    return factor_of


def noise(stream_key, shape, scale, reach, shards=(), held_as=jnp.bfloat16):
    entries = scale * jax.random.normal(stream_key, shape, jnp.float32)
    if shards:
        entries = entries * block_levels(stream_key, shape, shards, -0.22, 0.18)
    return jnp.clip(entries, -reach, reach).astype(held_as)


def setup_inputs(seed: int = 0) -> dict:
    arg_keys = jax.random.split(jax.random.key(seed), 6)
    tracers = noise(arg_keys[0], (TRACERS, LEV, NX, NY), 1.0, 6.0, ((2, 8), (3, 16)), jnp.float32)
    group_dest = draw_group_dest(jax.random.fold_in(arg_keys[5], 71), 0)
    group_slot = draw_group_slot(jax.random.fold_in(arg_keys[5], 71), 0)
    diffusivity = jnp.clip(jnp.exp(math.log(5.0) - 4.6051702 * jax.random.uniform(arg_keys[3], (LEV, NCHUNK), jnp.float32) ** block_levels(arg_keys[3], (LEV, NCHUNK), ((1, 128),), -0.2, 0.2)), 0.05, 5.0)
    surface_flux = noise(arg_keys[4], (TRACERS, NCHUNK), 1.0, 6.0, ((1, 128),), jnp.float32)
    return {"tracers": tracers, "group_dest": group_dest, "group_slot": group_slot, "diffusivity": diffusivity, "surface_flux": surface_flux}


hyper_rate = 0.025


def column_solve(columns, column_kv, column_flux):
    zero_row = jnp.zeros_like(column_kv[:1])
    upper_rate = jnp.concatenate([zero_row, column_kv[:-1]], 0)
    lower_rate = jnp.concatenate([column_kv[:-1], zero_row], 0)
    surface_drag = jnp.concatenate([jnp.zeros_like(column_kv[:-1]), column_kv[-1:]], 0)
    diagonal = 1.0 + upper_rate + lower_rate + surface_drag
    source = jnp.concatenate([columns[:, :-1], columns[:, -1:] + column_flux[:, None]], 1)
    levels_first = jnp.moveaxis(source, 1, 0)

    def forward(carried, level_items):
        ratio_prev, partial_prev = carried
        above_rate, below_rate, middle, right_side = level_items
        pivot_value = middle - above_rate * ratio_prev
        ratio_next = below_rate / pivot_value
        partial_next = (right_side + above_rate * partial_prev) / pivot_value
        return (ratio_next, partial_next), (ratio_next, partial_next)

    initial = (jnp.zeros_like(column_kv[0]), jnp.zeros_like(source[:, 0]))
    _, (ratios, partials) = lax.scan(forward, initial, (upper_rate, lower_rate, diagonal, levels_first))

    def backward(next_value, level_items):
        ratio_here, partial_here = level_items
        solved = partial_here + ratio_here * next_value
        return solved, solved

    _, solved_levels = lax.scan(backward, jnp.zeros_like(source[:, 0]), (ratios, partials), reverse=True)
    return jnp.moveaxis(solved_levels, 0, 1) - columns


def laplace(field):
    return jnp.roll(field, -1, 2) + jnp.roll(field, 1, 2) + jnp.roll(field, -1, 3) + jnp.roll(field, 1, 3) - 4.0 * field


def reference(tracers, group_dest, group_slot, diffusivity, surface_flux):
    phys_index = group_dest * (CX * CY) + group_slot

    def row_block(block_number):
        rows_state = lax.dynamic_slice_in_dim(tracers, block_number * CX, CX, 2)
        places = lax.dynamic_slice_in_dim(phys_index, block_number * CX, CX, 0)
        column_kv = jnp.take(diffusivity, places, axis=1)
        column_flux = jnp.take(surface_flux, places, axis=1)
        return rows_state + column_solve(rows_state, column_kv, column_flux)

    blocks = lax.map(row_block, jnp.arange(N_FX, dtype=jnp.int32))
    updated = jnp.moveaxis(blocks, 0, 2).reshape(TRACERS, LEV, NX, NY)
    return updated - hyper_rate * laplace(laplace(updated))
```

```python
import jax
import jax.numpy as jnp
from jax import lax
from jax.experimental import pallas as pl
from jax.experimental.pallas import tpu as pltpu
from jax.sharding import PartitionSpec as P

MESH = pl.DeviceIdType.MESH
F32 = jnp.float32
BF16 = jnp.bfloat16
CAP = 6
N_FX, N_FY, DEV = 8, 16, 128
TR, LEV, CX, CY = 8, 72, 16, 128
SLOTS = 2048
VALS = LEV + TR
STRIDE = 24
UROWS = TR * STRIDE + 8


def iota(shape, dim):
    return lax.broadcasted_iota(jnp.int32, shape, dim)


def split2(x):
    hi = x.astype(BF16)
    lo = (x - hi.astype(F32)).astype(BF16)
    return hi, lo


def split3(x):
    hi = x.astype(BF16)
    rest = x - hi.astype(F32)
    mid = rest.astype(BF16)
    lo = (rest - mid.astype(F32)).astype(BF16)
    return hi, mid, lo


def peer_at(step, fx, fy):
    z, core = fx // 2, fx % 2
    x, y = fy // 4, fy % 4
    dz = (2 + 3 * (step // 32)) % 4
    dx = (2 + 3 * ((step // 8) % 4)) % 4
    dy = (2 + 3 * ((step // 2) % 4)) % 4
    dc = (step + 1) % 2
    px = ((z + dz) % 4) * 2 + (core + dc) % 2
    py = ((x + dx) % 4) * 4 + (y + dy) % 4
    return px, py


SELF_STEP = 2 * 32 + 2 * 8 + 2 * 2 + 1


def each_peer(action, fx, fy):
    def one(step, carry):
        action(*peer_at(step, fx, fy))
        return carry

    lax.fori_loop(0, SELF_STEP, one, 0)
    lax.fori_loop(SELF_STEP + 1, DEV, one, 0)


def exchange_kernel(
    tracers, dest, slot, diff, flux,
    ue, us,
    tv, dest_v, slot_v, table, table_t, onehot, onehot_own, rank_v,
    req, req_in, rep, rep_in, dsplit, kv_own, kv, edge_kv, edge_kv_in, kv_halo,
    halo, edge, edge_in, edge_all, edge_kv_all, ratio_own, ratio_halo, ratio_side,
    load_sem, tv_sem, req_s, req_r, rep_s, rep_r, row_s, row_r, edge_s, edge_r,
    kvrow_s, kvrow_r, kvedge_s, kvedge_r,
):
    fx, fy = lax.axis_index("fx"), lax.axis_index("fy")
    me = fx * N_FY + fy
    up, down = (fx + N_FX - 1) % N_FX, (fx + 1) % N_FX
    left, right = (fy + N_FY - 1) % N_FY, (fy + 1) % N_FY

    loads = [
        pltpu.make_async_copy(dest, dest_v, load_sem.at[0]),
        pltpu.make_async_copy(slot, slot_v, load_sem.at[1]),
        pltpu.make_async_copy(diff, table.at[pl.ds(0, LEV)], load_sem.at[2]),
        pltpu.make_async_copy(flux, table.at[pl.ds(LEV, TR)], load_sem.at[3]),
    ]
    for load in loads:
        load.start()
    tv_load = pltpu.make_async_copy(tracers, tv, tv_sem)
    tv_load.start()

    barrier = pltpu.get_barrier_semaphore()

    def hello(px, py):
        pl.semaphore_signal(barrier, inc=1, device_id=(px, py), device_id_type=MESH)

    each_peer(hello, fx, fy)

    loads[0].wait()
    loads[1].wait()
    lane128 = iota((DEV, CY), 1)
    sub128 = iota((DEV, CY), 0)
    prefix = jnp.concatenate(
        [jnp.where(sub128 < lane128, 1.0, 0.0), jnp.ones((DEV, CY), F32)], 1
    ).astype(BF16)

    kk = iota((16, CY), 0)

    def route(i, carry):
        seen, asked = carry
        d = dest_v[pl.ds(i, 1), :]
        d = jnp.where(d == me, -1, d)
        code = slot_v[pl.ds(i, 1), :] + 1
        match = jnp.where(d == sub128, 1.0, 0.0)
        mb = match.astype(BF16)
        counts = jnp.dot(mb, prefix, preferred_element_type=F32)
        rank = jnp.sum(match * (counts[:, :CY] + seen), axis=0, keepdims=True)
        rank_v[pl.ds(i, 1), :] = rank
        value = jnp.where(kk < 8, code >> 7, code & 127).astype(F32)
        pick = jnp.where((kk & 7).astype(F32) == rank, value, 0.0).astype(BF16)
        asked = asked + lax.dot_general(
            mb, pick, (((1,), (1,)), ((), ())), preferred_element_type=F32
        )
        return seen + counts[:, CY:], asked

    _, asked = lax.fori_loop(
        0, CX, route, (jnp.zeros((DEV, CY), F32), jnp.zeros((DEV, 16), F32))
    )
    codes = asked[:, 0:8] * 128.0 + asked[:, 8:16]
    req[:, 0, :] = jnp.concatenate([codes, jnp.zeros((DEV, CY - 8), F32)], 1)

    pl.semaphore_wait(barrier, DEV - 1)

    def ask(px, py):
        pltpu.make_async_remote_copy(
            req.at[px * N_FY + py], req_in.at[me], req_s, req_r,
            device_id=(px, py), device_id_type=MESH,
        ).start()

    each_peer(ask, fx, fy)
    req_in[me] = jnp.zeros((1, CY), F32)

    rows = []
    for t in range(TR):
        rows.append(
            pltpu.make_async_remote_copy(
                tracers.at[t, :, pl.ds(14, 2), :],
                halo.at[:, pl.ds(8 * t + 6, 2), :],
                row_s.at[t], row_r.at[t], device_id=(down, fy), device_id_type=MESH,
            )
        )
        rows.append(
            pltpu.make_async_remote_copy(
                tracers.at[t, :, pl.ds(0, 2), :],
                halo.at[:, pl.ds(8 * t + 8, 2), :],
                row_s.at[TR + t], row_r.at[TR + t], device_id=(up, fy), device_id_type=MESH,
            )
        )
    for copy in rows:
        copy.start()

    loads[2].wait()
    loads[3].wait()

    def flip(b, carry):
        cols = pl.ds(pl.multiple_of(b * 128, 128), 128)
        part = jnp.concatenate([table[:, cols], jnp.zeros((128 - VALS, 128), F32)], 0)
        hi, lo = split2(part.T)
        table_t[cols, pl.ds(0, 128)] = hi
        table_t[cols, pl.ds(128, 128)] = lo
        return carry

    lax.fori_loop(0, SLOTS // 128, flip, 0)

    pltpu.make_async_copy(req_in.at[pl.ds(0, DEV - 1)], req_in.at[pl.ds(0, DEV - 1)], req_r).wait()
    wanted = req_in[:, 0, :]
    slot_lane = (iota((DEV, SLOTS), 1) + 1).astype(F32)
    got = []
    for k in range(CAP):
        pick = jnp.where(wanted[:, k : k + 1] == slot_lane, 1.0, 0.0).astype(BF16)
        both = jnp.dot(pick, table_t[...], preferred_element_type=F32)
        got.append(both[:, :128] + both[:, 128:])
    for j in range(3):
        rep[:, j, :] = jnp.where(lane128 < 64, got[2 * j], pltpu.roll(got[2 * j + 1], 64, 1))
    tail = jnp.zeros((DEV, CY), F32)
    for k in range(CAP):
        shift = (16 * k - 64) % 128
        moved = pltpu.roll(got[k], shift, 1) if shift else got[k]
        tail = jnp.where(lane128 // 16 == k, moved, tail)
    rep[:, 3, :] = tail

    def answer(px, py):
        pltpu.make_async_remote_copy(
            rep.at[px * N_FY + py], rep_in.at[me], rep_s, rep_r,
            device_id=(px, py), device_id_type=MESH,
        ).start()

    each_peer(answer, fx, fy)
    rep_in[me] = jnp.zeros((4, CY), F32)

    tv_load.wait()
    lane16 = iota((CX, CY), 1)

    def pack(q, carry):
        acc = jnp.zeros((CX, CY), F32)
        for lg in range(4):
            for t in range(TR):
                cells = tv[t, q + 18 * lg]
                at = 32 * lg + 4 * t
                first = pltpu.roll(cells, at, 1) if at else cells
                last = pltpu.roll(cells, (at + 4) % 128, 1) if (at + 4) % 128 else cells
                acc = jnp.where((lane16 == at) | (lane16 == at + 1), first, acc)
                acc = jnp.where((lane16 == at + 2) | (lane16 == at + 3), last, acc)
        edge[q] = acc
        return carry

    lax.fori_loop(0, 18, pack, 0)

    def to_sides(source, target, sends, receives):
        places = [
            (fx, right, 0, 0, 16), (fx, left, 1, 0, 16),
            (down, right, 2, 8, 8), (down, left, 3, 8, 8),
            (up, right, 4, 0, 8), (up, left, 5, 0, 8),
        ]
        copies = [
            pltpu.make_async_remote_copy(
                source.at[:, pl.ds(first, count), :],
                target.at[n, :, pl.ds(first, count), :],
                sends.at[n], receives.at[n], device_id=(px, py), device_id_type=MESH,
            )
            for px, py, n, first, count in places
        ]
        for copy in copies:
            copy.start()
        return copies

    edges = to_sides(edge, edge_in, edge_s, edge_r)

    def spread(i, carry):
        cols = pl.ds(pl.multiple_of(i * CY, CY), CY)
        d = dest_v[pl.ds(i, 1), :]
        d = jnp.where(d == me, -1, d)
        rank = rank_v[pl.ds(i, 1), :]
        hit = d == sub128
        for k in range(CAP):
            onehot[pl.ds(k * DEV, DEV), cols] = jnp.where(
                hit & (rank == float(k)), 1.0, 0.0
            ).astype(BF16)
        return carry

    lax.fori_loop(0, CX, spread, 0)
    slot_sub = iota((SLOTS, CY), 0)
    tab3 = jnp.concatenate(split3(table[...]), 0)

    def keep(i, carry):
        for half in range(2):
            d = dest_v[pl.ds(2 * i + half, 1), :]
            s = jnp.where(d == me, slot_v[pl.ds(2 * i + half, 1), :], -1)
            onehot_own[:, pl.ds(half * CY, CY)] = jnp.where(s == slot_sub, 1.0, 0.0).astype(BF16)
        three = jnp.dot(tab3, onehot_own[...], preferred_element_type=F32)
        kv_own[:, pl.ds(pl.multiple_of(i * 2 * CY, 2 * CY), 2 * CY)] = (
            three[:VALS] + three[VALS : 2 * VALS] + three[2 * VALS :]
        )
        return carry

    lax.fori_loop(0, CX // 2, keep, 0)

    pltpu.make_async_copy(rep_in.at[pl.ds(0, DEV - 1)], rep_in.at[pl.ds(0, DEV - 1)], rep_r).wait()
    last = rep_in[:, 3, :]
    for k in range(CAP):
        main = rep_in[:, k // 2, :]
        if k % 2:
            main = pltpu.roll(main, 64, 1)
        shift = (64 - 16 * k) % 128
        end = pltpu.roll(last, shift, 1) if shift else last
        cols = jnp.where(lane128 < 64, main, jnp.where(lane128 < VALS, end, 0.0))
        hi, lo = split2(cols.T[:VALS])
        dsplit[pl.ds(0, VALS), pl.ds(k * DEV, DEV)] = hi
        dsplit[pl.ds(VALS, VALS), pl.ds(k * DEV, DEV)] = lo

    def assemble(i, carry):
        cols = pl.ds(pl.multiple_of(i * 2 * CY, 2 * CY), 2 * CY)
        two = jnp.dot(dsplit[...], onehot[:, cols], preferred_element_type=F32)
        full = kv_own[:, cols] + two[:VALS] + two[VALS:]
        kv[:, 2 * i, :] = full[:, :CY]
        kv[:, 2 * i + 1, :] = full[:, CY:]
        return carry

    for i in range(CX // 2):
        assemble(i, 0)

    kvrows = [
        pltpu.make_async_remote_copy(
            kv.at[:, pl.ds(14, 2), :], kv_halo.at[:, pl.ds(6, 2), :],
            kvrow_s.at[0], kvrow_r.at[0], device_id=(down, fy), device_id_type=MESH,
        ),
        pltpu.make_async_remote_copy(
            kv.at[:, pl.ds(0, 2), :], kv_halo.at[:, pl.ds(0, 2), :],
            kvrow_s.at[1], kvrow_r.at[1], device_id=(up, fy), device_id_type=MESH,
        ),
    ]
    for copy in kvrows:
        copy.start()
    for g in range(3):
        acc = jnp.zeros((CX, CY), F32)
        for m in range(32 if g < 2 else VALS - 64):
            moved = pltpu.roll(kv[32 * g + m], 4 * m + 2, 1) if 4 * m + 2 < 128 else kv[32 * g + m]
            acc = jnp.where(lane16 // 4 == m, moved, acc)
        edge_kv[g] = acc
    kvedges = to_sides(edge_kv, edge_kv_in, kvedge_s, kvedge_r)

    def factors(level, above_kv, here_kv, ratio):
        inner = (level < LEV - 1).astype(F32)
        above = above_kv * (level > 0).astype(F32)
        below = here_kv * inner
        pivot = 1.0 + above + here_kv - above * ratio
        inverse = 1.0 / pivot
        return below * inverse, inverse, above

    def forward(level, carry):
        ratio, partial = carry
        ratio, inverse, above = factors(level, kv[jnp.maximum(level - 1, 0)], kv[level], ratio)
        ratio_own[level] = ratio
        bottom = (level == LEV - 1).astype(F32)
        new = []
        for t in range(TR):
            g = (tv[t, level] + kv[LEV + t] * bottom + above * partial[t]) * inverse
            ue[level, pl.ds(STRIDE * t + 8, CX), :] = g
            new.append(g)
        return ratio, tuple(new)

    zero16 = jnp.zeros((CX, CY), F32)
    lax.fori_loop(0, LEV, forward, (zero16, (zero16,) * TR))

    def backward(step, below):
        level = LEV - 1 - step
        ratio = ratio_own[level]
        new = []
        for t in range(TR):
            rows_t = pl.ds(STRIDE * t + 8, CX)
            x = ue[level, rows_t, :] + ratio * below[t]
            ue[level, rows_t, :] = x
            new.append(x)
        return tuple(new)

    lax.fori_loop(0, LEV, backward, (zero16,) * TR)

    for copy in rows + edges:
        copy.wait_recv()
    lane8 = iota((8, CY), 1)
    sub8 = iota((8, CY), 0)

    def gather_edges(q, carry):
        edge_all[q, pl.ds(0, CX), :] = jnp.where(lane16 % 4 < 2, edge_in[1, q], edge_in[0, q])
        above = jnp.where(lane8 % 4 < 2, edge_in[3, q, pl.ds(8, 8)], edge_in[2, q, pl.ds(8, 8)])
        below = jnp.where(lane8 % 4 < 2, edge_in[5, q, pl.ds(0, 8)], edge_in[4, q, pl.ds(0, 8)])
        edge_all[q, pl.ds(CX, 8), :] = jnp.where(sub8 == 7, above, below)
        return carry

    lax.fori_loop(0, 18, gather_edges, 0)
    for copy in kvrows + kvedges:
        copy.wait_recv()
    for g in range(3):
        edge_kv_all[g, pl.ds(0, CX), :] = jnp.where(lane16 % 4 < 2, edge_kv_in[0, g], edge_kv_in[1, g])
        above = jnp.where(lane8 % 4 < 2, edge_kv_in[2, g, pl.ds(8, 8)], edge_kv_in[3, g, pl.ds(8, 8)])
        below = jnp.where(lane8 % 4 < 2, edge_kv_in[4, g, pl.ds(0, 8)], edge_kv_in[5, g, pl.ds(0, 8)])
        edge_kv_all[g, pl.ds(CX, 8), :] = jnp.where(sub8 == 7, above, below)

    lane24 = iota((24, CY), 1)
    quad = (lane24 + 2) % 4

    def side_kv(level):
        source = edge_kv_all[level // 32]
        return jnp.take_along_axis(source, 4 * (level % 32) + quad, axis=1)

    side_flux = jnp.take_along_axis(
        edge_kv_all[2], 32 + 4 * ((lane24 // 4) % 8) + quad, axis=1
    )

    def forward_rim(level, carry):
        ratio, partial, sratio, spartial, kv_above = carry
        bottom = (level == LEV - 1).astype(F32)
        ratio, inverse, above = factors(
            level, kv_halo[jnp.maximum(level - 1, 0)], kv_halo[level], ratio
        )
        ratio_halo[level] = ratio
        new = []
        for j in range(TR + 1):
            source = jnp.where(
                sub8 < 4, kv_halo[LEV + max(j - 1, 0)], kv_halo[LEV + min(j, TR - 1)]
            )
            g = (halo[level, pl.ds(8 * j, 8), :] + source * bottom + above * partial[j]) * inverse
            ue[level, pl.ds(STRIDE * j, 8), :] = g
            new.append(g)
        kv_here = side_kv(level)
        sratio, inverse, above = factors(level, kv_above, kv_here, sratio)
        ratio_side[level] = sratio
        raw = pltpu.roll(edge_all[level % 18], (128 - 32 * (level // 18)) % 128, 1)
        g = (raw + side_flux * bottom + above * spartial) * inverse
        us[level, pl.ds(8, 24), :] = g
        return ratio, tuple(new), sratio, g, kv_here

    zero8 = jnp.zeros((8, CY), F32)
    zero24 = jnp.zeros((24, CY), F32)
    lax.fori_loop(0, LEV, forward_rim, (zero8, (zero8,) * (TR + 1), zero24, zero24, zero24))

    def backward_rim(step, carry):
        level = LEV - 1 - step
        below, sbelow = carry
        ratio = ratio_halo[level]
        new = []
        for j in range(TR + 1):
            rows_j = pl.ds(STRIDE * j, 8)
            x = ue[level, rows_j, :] + ratio * below[j]
            ue[level, rows_j, :] = x
            new.append(x)
        x = us[level, pl.ds(8, 24), :] + ratio_side[level] * sbelow
        us[level, pl.ds(8, 24), :] = x
        us[level, pl.ds(0, 8), :] = x[16:24]
        return tuple(new), x

    lax.fori_loop(0, LEV, backward_rim, ((zero8,) * (TR + 1), zero24))

    for copy in rows + edges + kvrows + kvedges:
        copy.wait_send()
    pltpu.make_async_copy(req.at[pl.ds(0, DEV - 1)], req.at[pl.ds(0, DEV - 1)], req_s).wait()
    pltpu.make_async_copy(rep.at[pl.ds(0, DEV - 1)], rep.at[pl.ds(0, DEV - 1)], rep_s).wait()


def smooth_kernel(ue, us, out):
    block = pl.program_id(0)
    count = out.shape[1]
    lane = iota((CX, CY), 1)
    place = lane % 4
    rim = (lane < 2) | (lane >= CY - 2)

    def one(n, carry):
        level = block * count + n
        u = us[level, pl.ds(8, CX), :]
        p = 0.2 * u - 0.05 * (us[level, pl.ds(7, CX), :] + us[level, pl.ds(9, CX), :])
        cross = jnp.where(
            place == 1, pltpu.roll(p, 1, 1), jnp.where(place == 2, pltpu.roll(p, CY - 1, 1), 0.0)
        )
        side = cross - 0.025 * u
        for t in range(TR):
            row = STRIDE * t + 8
            u = ue[level, pl.ds(row, CX), :]
            near = ue[level, pl.ds(row - 1, CX), :] + ue[level, pl.ds(row + 1, CX), :]
            far = ue[level, pl.ds(row - 2, CX), :] + ue[level, pl.ds(row + 2, CX), :]
            p = 0.2 * u - 0.05 * near
            s = -0.025 * u
            west = p + jnp.where(lane == 0, 0.0, pltpu.roll(s, 1, 1))
            east = p + jnp.where(lane == CY - 1, 0.0, pltpu.roll(s, CY - 1, 1))
            west = jnp.where(lane == 0, 0.0, pltpu.roll(west, 1, 1))
            east = jnp.where(lane == CY - 1, 0.0, pltpu.roll(east, CY - 1, 1))
            outer = jnp.where(rim, pltpu.roll(side, (CY - 2 - 4 * t) % CY, 1), 0.0)
            out[t, n] = 0.5 * u + 0.2 * near - 0.025 * far + (west + east) + outer
        return carry

    lax.fori_loop(0, count, one, 0)


def local(tracers, group_dest, group_slot, diffusivity, surface_flux):
    any_spec = pl.BlockSpec(memory_space=pl.ANY)
    dma = pltpu.SemaphoreType.DMA
    ue, us = pl.pallas_call(
        exchange_kernel,
        out_shape=(
            pltpu.VMEM((LEV, UROWS, CY), F32),
            pltpu.VMEM((LEV, 32, CY), F32),
        ),
        in_specs=[any_spec] * 5,
        out_specs=(pl.BlockSpec(memory_space=pltpu.VMEM), pl.BlockSpec(memory_space=pltpu.VMEM)),
        scratch_shapes=[
            pltpu.VMEM((TR, LEV, CX, CY), F32),
            pltpu.VMEM((CX, CY), jnp.int32),
            pltpu.VMEM((CX, CY), jnp.int32),
            pltpu.VMEM((VALS, SLOTS), F32),
            pltpu.VMEM((SLOTS, 256), BF16),
            pltpu.VMEM((CAP * DEV, SLOTS), BF16),
            pltpu.VMEM((SLOTS, 256), BF16),
            pltpu.VMEM((CX, CY), F32),
            pltpu.VMEM((DEV, 1, CY), F32),
            pltpu.VMEM((DEV, 1, CY), F32),
            pltpu.VMEM((DEV, 4, CY), F32),
            pltpu.VMEM((DEV, 4, CY), F32),
            pltpu.VMEM((2 * VALS, CAP * DEV), BF16),
            pltpu.VMEM((VALS, SLOTS), F32),
            pltpu.VMEM((VALS, CX, CY), F32),
            pltpu.VMEM((3, CX, CY), F32),
            pltpu.VMEM((6, 3, CX, CY), F32),
            pltpu.VMEM((VALS, 8, CY), F32),
            pltpu.VMEM((LEV, 8 * (TR + 1), CY), F32),
            pltpu.VMEM((18, CX, CY), F32),
            pltpu.VMEM((6, 18, CX, CY), F32),
            pltpu.VMEM((18, 24, CY), F32),
            pltpu.VMEM((3, 24, CY), F32),
            pltpu.VMEM((LEV, CX, CY), F32),
            pltpu.VMEM((LEV, 8, CY), F32),
            pltpu.VMEM((LEV, 24, CY), F32),
            dma((4,)), dma, dma, dma, dma, dma,
            dma((2 * TR,)), dma((2 * TR,)), dma((6,)), dma((6,)),
            dma((2,)), dma((2,)), dma((6,)), dma((6,)),
        ],
        compiler_params=pltpu.CompilerParams(
            collective_id=0, has_side_effects=True, vmem_limit_bytes=44 << 20
        ),
        name="exchange",
    )(tracers, group_dest, group_slot, diffusivity, surface_flux)
    count = 9
    whole = pl.BlockSpec(memory_space=pltpu.VMEM)
    return pl.pallas_call(
        smooth_kernel,
        grid=(LEV // count,),
        out_shape=jax.ShapeDtypeStruct(tracers.shape, F32),
        in_specs=[whole, whole],
        out_specs=pl.BlockSpec((TR, count, CX, CY), lambda b: (0, b, 0, 0)),
        compiler_params=pltpu.CompilerParams(vmem_limit_bytes=20 << 20),
        name="smooth",
    )(ue, us)


def solution(mesh):
    placed = (
        P(None, None, "fx", "fy"),
        P("fx", "fy"),
        P("fx", "fy"),
        P(None, ("fx", "fy")),
        P(None, ("fx", "fy")),
    )
    return jax.shard_map(
        local, mesh=mesh, in_specs=placed, out_specs=P(None, None, "fx", "fy"), check_vma=False
    )
```

```python
import jax
import jax.numpy as jnp
from jax import lax
from jax.experimental import pallas as pl
from jax.experimental.pallas import tpu as pltpu
from jax.sharding import PartitionSpec as P

MESH = pl.DeviceIdType.MESH
F32 = jnp.float32
BF16 = jnp.bfloat16
CAP = 6
N_FX, N_FY, DEV = 8, 16, 128
TR, LEV, CX, CY = 8, 72, 16, 128
SLOTS = 2048
VALS = LEV + TR
STRIDE = 24
UROWS = TR * STRIDE + 8


def iota(shape, dim):
    return lax.broadcasted_iota(jnp.int32, shape, dim)


def split2(x):
    hi = x.astype(BF16)
    lo = (x - hi.astype(F32)).astype(BF16)
    return hi, lo


def split3(x):
    hi = x.astype(BF16)
    rest = x - hi.astype(F32)
    mid = rest.astype(BF16)
    lo = (rest - mid.astype(F32)).astype(BF16)
    return hi, mid, lo


HOPS = (0, 1, 2, 1)
STEPS = sorted(
    (
        (dz, dx, dy, dc)
        for dz in range(4) for dx in range(4) for dy in range(4) for dc in range(2)
        if dz or dx or dy or dc
    ),
    key=lambda d: -(HOPS[d[0]] + HOPS[d[1]] + HOPS[d[2]]),
)


def all_peers(fx, fy):
    z, core, x, y = fx // 2, fx % 2, fy // 4, fy % 4
    zs, cores = [(z + d) % 4 * 2 for d in range(4)], [core, 1 - core]
    xs, ys = [(x + d) % 4 * 4 for d in range(4)], [(y + d) % 4 for d in range(4)]
    on_fx = {(dz, dc): zs[dz] + cores[dc] for dz in range(4) for dc in range(2)}
    on_fy = {(dx, dy): xs[dx] + ys[dy] for dx in range(4) for dy in range(4)}
    return [(on_fx[dz, dc], on_fy[dx, dy]) for dz, dx, dy, dc in STEPS]


def exchange_kernel(
    tracers, dest, slot, diff, flux,
    ue, us,
    tv, dest_v, slot_v, table, table_t, onehot, onehot_own, rank_v,
    matches, picks, chosen, widen, req, req_in, rep, rep_in, dsplit, kv_own, kv, edge_kv, edge_kv_in, kv_halo,
    halo, edge, edge_in, side_raw, side_kv, edge_kv_all, ratio_own, ratio_halo, ratio_side,
    load_sem, tv_sem, req_s, req_r, rep_s, rep_r, row_s, row_r, edge_s, edge_r,
    kvrow_s, kvrow_r, kvedge_s, kvedge_r,
):
    fx, fy = lax.axis_index("fx"), lax.axis_index("fy")
    me = fx * N_FY + fy
    up, down = (fx + N_FX - 1) % N_FX, (fx + 1) % N_FX
    left, right = (fy + N_FY - 1) % N_FY, (fy + 1) % N_FY

    loads = [
        pltpu.make_async_copy(dest, dest_v, load_sem.at[0]),
        pltpu.make_async_copy(slot, slot_v, load_sem.at[1]),
        pltpu.make_async_copy(diff, table.at[pl.ds(0, LEV)], load_sem.at[2]),
        pltpu.make_async_copy(flux, table.at[pl.ds(LEV, TR)], load_sem.at[3]),
    ]
    for load in loads:
        load.start()
    tv_load = pltpu.make_async_copy(tracers, tv, tv_sem)
    tv_load.start()

    barrier = pltpu.get_barrier_semaphore()
    peers = all_peers(fx, fy)

    def each_peer(action):
        for px, py in peers:
            action(px, py)

    def hello(px, py):
        pl.semaphore_signal(barrier, inc=1, device_id=(px, py), device_id_type=MESH)

    each_peer(hello)

    loads[0].wait()
    loads[1].wait()
    lane128 = iota((DEV, CY), 1)
    sub128 = iota((DEV, CY), 0)
    prefix = jnp.concatenate(
        [jnp.where(sub128 < lane128, 1.0, 0.0), jnp.ones((DEV, CY), F32)], 1
    ).astype(BF16)

    kk = iota((16, CY), 0)
    seen = jnp.zeros((DEV, CY), F32)
    for i in range(CX):
        d = dest_v[pl.ds(i, 1), :]
        d = jnp.where(d == me, -1, d)
        slots = slot_v[pl.ds(i, 1), :]
        match = jnp.where(d == sub128, 1.0, 0.0)
        mb = match.astype(BF16)
        matches[:, pl.ds(i * CY, CY)] = mb
        counts = jnp.dot(mb, prefix, preferred_element_type=F32)
        rank = jnp.sum(match * (counts[:, :CY] + seen), axis=0, keepdims=True)
        seen = seen + counts[:, CY:]
        rank_v[pl.ds(i, 1), :] = rank
        value = jnp.where(kk < 8, (slots >> 7) + 1, slots & 127).astype(F32)
        picks[:, pl.ds(i * CY, CY)] = jnp.where((kk & 7).astype(F32) == rank, value, 0.0).astype(BF16)
    asked = lax.dot_general(
        matches[...], picks[...], (((1,), (1,)), ((), ())), preferred_element_type=F32
    )
    req[:, 0, :] = jnp.concatenate([asked, jnp.zeros((DEV, CY - 16), F32)], 1)

    loads[2].wait()
    loads[3].wait()

    def flip(b, carry):
        cols = pl.ds(pl.multiple_of(b * 128, 128), 128)
        part = jnp.concatenate([table[:, cols], jnp.zeros((128 - VALS, 128), F32)], 0)
        hi, lo = split2(part.T)
        table_t[cols, pl.ds(0, 128)] = hi
        table_t[cols, pl.ds(128, 128)] = lo
        return carry

    lax.fori_loop(0, SLOTS // 128, flip, 0)

    for m in range(2 * CAP):
        lane_of = m if m < CAP else 8 + m - CAP
        widen[:, pl.ds(m * CY, CY)] = jnp.where(sub128 == lane_of, 1.0, 0.0).astype(BF16)

    def spread(i, carry):
        cols = pl.ds(pl.multiple_of(i * CY, CY), CY)
        d = dest_v[pl.ds(i, 1), :]
        d = jnp.where(d == me, -1, d)
        rank = rank_v[pl.ds(i, 1), :]
        hit = d == sub128
        for k in range(CAP):
            onehot[pl.ds(k * DEV, DEV), cols] = jnp.where(
                hit & (rank == float(k)), 1.0, 0.0
            ).astype(BF16)
        return carry

    lax.fori_loop(0, CX, spread, 0)
    pl.semaphore_wait(barrier, DEV - 1)

    def ask(px, py):
        pltpu.make_async_remote_copy(
            req.at[px * N_FY + py], req_in.at[me], req_s, req_r,
            device_id=(px, py), device_id_type=MESH,
        ).start()

    each_peer(ask)
    req_in[me] = jnp.zeros((1, CY), F32)

    rows = []
    for t in range(TR):
        rows.append(
            pltpu.make_async_remote_copy(
                tracers.at[t, :, pl.ds(14, 2), :],
                halo.at[:, pl.ds(8 * t + 6, 2), :],
                row_s.at[t], row_r.at[t], device_id=(down, fy), device_id_type=MESH,
            )
        )
        rows.append(
            pltpu.make_async_remote_copy(
                tracers.at[t, :, pl.ds(0, 2), :],
                halo.at[:, pl.ds(8 * t + 8, 2), :],
                row_s.at[TR + t], row_r.at[TR + t], device_id=(up, fy), device_id_type=MESH,
            )
        )
    for copy in rows:
        copy.start()

    tv_load.wait()
    lane16 = iota((CX, CY), 1)

    def pack(q, carry):
        first = last = jnp.zeros((CX, CY), F32)
        for lg in range(8):
            for t in range(TR):
                cells = tv[t, q + 9 * lg]
                at = 16 * lg + 2 * t
                here = (lane16 == at) | (lane16 == at + 1)
                first = jnp.where(here, pltpu.roll(cells, at, 1) if at else cells, first)
                moved = pltpu.roll(cells, (at + 2) % 128, 1) if (at + 2) % 128 else cells
                last = jnp.where(here, moved, last)
        edge[0, q] = last
        edge[1, q] = first
        return carry

    lax.fori_loop(0, 9, pack, 0)

    def to_sides(sources, target, sends, receives):
        places = [
            (fx, right, 0, 0, CX), (fx, left, 1, 0, CX),
            (down, right, 2, CX - 1, 1), (down, left, 3, CX - 1, 1),
            (up, right, 4, 0, 1), (up, left, 5, 0, 1),
        ]
        copies = [
            pltpu.make_async_remote_copy(
                sources[n % 2].at[:, pl.ds(first, count), :],
                target.at[n, :, pl.ds(first, count), :],
                sends.at[n], receives.at[n], device_id=(px, py), device_id_type=MESH,
            )
            for px, py, n, first, count in places
        ]
        for copy in copies:
            copy.start()
        return copies

    edges = to_sides((edge.at[0], edge.at[1]), edge_in, edge_s, edge_r)

    pltpu.make_async_copy(req_in.at[pl.ds(0, DEV - 1)], req_in.at[pl.ds(0, DEV - 1)], req_r).wait()
    wanted = req_in[:, 0, :]
    zero_b = jnp.zeros((DEV, CY), BF16)
    zero_f = jnp.zeros((DEV, CY), F32)
    lane_f = lane128.astype(F32)
    apart = jnp.dot(wanted.astype(BF16), widen[...], preferred_element_type=F32)
    for k in range(CAP):
        high = apart[:, k * CY : (k + 1) * CY].astype(BF16)
        low = jnp.where(apart[:, (CAP + k) * CY : (CAP + k + 1) * CY] == lane_f, 1.0, 0.0).astype(BF16)
        for b in range(SLOTS // 128):
            chosen[pl.ds(k * DEV, DEV), pl.ds(b * 128, 128)] = jnp.where(high == float(b + 1), low, zero_b)
    both = jnp.dot(chosen[...], table_t[...], preferred_element_type=F32)
    both = both[:, :128] + both[:, 128:]
    got = [both[k * DEV : (k + 1) * DEV] for k in range(CAP)]
    for j in range(3):
        rep[:, j, :] = jnp.where(lane128 < 64, got[2 * j], pltpu.roll(got[2 * j + 1], 64, 1))
    tail = jnp.zeros((DEV, CY), F32)
    for k in range(CAP):
        shift = (16 * k - 64) % 128
        moved = pltpu.roll(got[k], shift, 1) if shift else got[k]
        tail = jnp.where(lane128 // 16 == k, moved, tail)
    rep[:, 3, :] = tail

    def answer(px, py):
        pltpu.make_async_remote_copy(
            rep.at[px * N_FY + py], rep_in.at[me], rep_s, rep_r,
            device_id=(px, py), device_id_type=MESH,
        ).start()

    each_peer(answer)
    rep_in[me] = jnp.zeros((4, CY), F32)

    tab3 = jnp.concatenate(split3(table[...]), 0)

    def keep(i, carry):
        for half in range(2):
            d = dest_v[pl.ds(2 * i + half, 1), :]
            s = jnp.where(d == me, slot_v[pl.ds(2 * i + half, 1), :], -1)
            high = ((s >> 7).astype(F32) + zero_f).astype(BF16)
            low = jnp.where((s & 127) == sub128, 1.0, 0.0).astype(BF16)
            for b in range(SLOTS // 128):
                onehot_own[pl.ds(b * 128, 128), pl.ds(half * CY, CY)] = jnp.where(
                    high == float(b), low, zero_b
                )
        three = jnp.dot(tab3, onehot_own[...], preferred_element_type=F32)
        kv_own[:, pl.ds(pl.multiple_of(i * 2 * CY, 2 * CY), 2 * CY)] = (
            three[:VALS] + three[VALS : 2 * VALS] + three[2 * VALS :]
        )
        return carry

    lax.fori_loop(0, CX // 2, keep, 0)

    for copy in edges:
        copy.wait_recv()
    lane8 = iota((8, CY), 1)
    sub8 = iota((8, CY), 0)
    lane24 = iota((24, CY), 1)

    def gather_edges(q, carry):
        def merged(n, rows):
            return edge_in[n + 1, q, rows], edge_in[n, q, rows]

        sides = merged(0, pl.ds(0, CX))
        over = merged(2, pl.ds(8, 8))
        under = merged(4, pl.ds(0, 8))
        right_cells, left_cells = (
            jnp.concatenate([a, jnp.where(sub8 == 7, b, c)], 0)
            for a, b, c in zip(sides, over, under)
        )
        for lg in range(8):
            near_r = pltpu.roll(right_cells, 128 - 16 * lg, 1) if lg else right_cells
            near_l = pltpu.roll(left_cells, (144 - 16 * lg) % 128, 1) if lg != 1 else left_cells
            side_raw[9 * lg + q] = jnp.where(lane24 < 16, near_r, near_l)
        return carry

    lax.fori_loop(0, 9, gather_edges, 0)

    pltpu.make_async_copy(rep_in.at[pl.ds(0, DEV - 1)], rep_in.at[pl.ds(0, DEV - 1)], rep_r).wait()
    last = rep_in[:, 3, :]
    for k in range(CAP):
        main = rep_in[:, k // 2, :]
        if k % 2:
            main = pltpu.roll(main, 64, 1)
        shift = (64 - 16 * k) % 128
        end = pltpu.roll(last, shift, 1) if shift else last
        cols = jnp.where(lane128 < 64, main, jnp.where(lane128 < VALS, end, 0.0))
        hi, lo = split2(cols.T[:VALS])
        dsplit[pl.ds(0, VALS), pl.ds(k * DEV, DEV)] = hi
        dsplit[pl.ds(VALS, VALS), pl.ds(k * DEV, DEV)] = lo

    def assemble(i, carry):
        cols = pl.ds(pl.multiple_of(i * 2 * CY, 2 * CY), 2 * CY)
        two = jnp.dot(dsplit[...], onehot[:, cols], preferred_element_type=F32)
        full = kv_own[:, cols] + two[:VALS] + two[VALS:]
        kv[:, 2 * i, :] = full[:, :CY]
        kv[:, 2 * i + 1, :] = full[:, CY:]
        return carry

    for i in range(CX // 2):
        assemble(i, 0)

    kvrows = [
        pltpu.make_async_remote_copy(
            kv.at[:, pl.ds(14, 2), :], kv_halo.at[:, pl.ds(6, 2), :],
            kvrow_s.at[0], kvrow_r.at[0], device_id=(down, fy), device_id_type=MESH,
        ),
        pltpu.make_async_remote_copy(
            kv.at[:, pl.ds(0, 2), :], kv_halo.at[:, pl.ds(0, 2), :],
            kvrow_s.at[1], kvrow_r.at[1], device_id=(up, fy), device_id_type=MESH,
        ),
    ]
    for copy in kvrows:
        copy.start()
    for g in range(3):
        acc = jnp.zeros((CX, CY), F32)
        for m in range(32 if g < 2 else VALS - 64):
            moved = pltpu.roll(kv[32 * g + m], 4 * m + 2, 1) if 4 * m + 2 < 128 else kv[32 * g + m]
            acc = jnp.where(lane16 // 4 == m, moved, acc)
        edge_kv[g] = acc
    kvedges = to_sides((edge_kv, edge_kv), edge_kv_in, kvedge_s, kvedge_r)

    def factors(kv_above, kv_here, share):
        rest = 1.0 + kv_above * share
        inverse = 1.0 / (rest + kv_here)
        return kv_here * inverse, inverse, rest * inverse

    zero16 = jnp.zeros((CX, CY), F32)
    ones16 = jnp.ones((CX, CY), F32)
    last_level = LEV - 1

    def forward(level, carry):
        above, share, partial = carry
        here = kv[level]
        ratio, inverse, share = factors(above, here, share)
        ratio_own[level] = ratio
        new = []
        for t in range(TR):
            g = (tv[t, level] + above * partial[t]) * inverse
            ue[level, pl.ds(STRIDE * t + 8, CX), :] = g
            new.append(g)
        return here, share, tuple(new)

    above, share, partial = lax.fori_loop(
        0, last_level, forward, (zero16, ones16, (zero16,) * TR)
    )
    _, inverse, _ = factors(above, kv[last_level], share)
    below = []
    for t in range(TR):
        x = (tv[t, last_level] + kv[LEV + t] + above * partial[t]) * inverse
        ue[last_level, pl.ds(STRIDE * t + 8, CX), :] = x
        below.append(x)

    def backward(step, below):
        level = last_level - 1 - step
        ratio = ratio_own[level]
        new = []
        for t in range(TR):
            rows_t = pl.ds(STRIDE * t + 8, CX)
            x = ue[level, rows_t, :] + ratio * below[t]
            ue[level, rows_t, :] = x
            new.append(x)
        return tuple(new)

    lax.fori_loop(0, last_level, backward, tuple(below))

    for copy in kvrows + kvedges:
        copy.wait_recv()
    for copy in rows:
        copy.wait_recv()
    for g in range(3):
        edge_kv_all[g, pl.ds(0, CX), :] = jnp.where(lane16 % 4 < 2, edge_kv_in[0, g], edge_kv_in[1, g])
        over = jnp.where(lane8 % 4 < 2, edge_kv_in[2, g, pl.ds(8, 8)], edge_kv_in[3, g, pl.ds(8, 8)])
        under = jnp.where(lane8 % 4 < 2, edge_kv_in[4, g, pl.ds(0, 8)], edge_kv_in[5, g, pl.ds(0, 8)])
        edge_kv_all[g, pl.ds(CX, 8), :] = jnp.where(sub8 == 7, over, under)
    quad = jnp.where(lane24 % 32 < 16, 2, 0) + lane24 % 2

    for level in range(LEV):
        side_kv[level] = jnp.take_along_axis(
            edge_kv_all[level // 32], 4 * (level % 32) + quad, axis=1
        )

    side_flux = jnp.take_along_axis(
        edge_kv_all[2], 32 + 4 * ((lane24 % 16) // 2) + quad, axis=1
    )

    def forward_rim(level, carry):
        above, share, partial, sabove, sshare, spartial = carry
        here = kv_halo[level]
        ratio, inverse, share = factors(above, here, share)
        ratio_halo[level] = ratio
        new = []
        for j in range(TR + 1):
            g = (halo[level, pl.ds(8 * j, 8), :] + above * partial[j]) * inverse
            ue[level, pl.ds(STRIDE * j, 8), :] = g
            new.append(g)
        shere = side_kv[level]
        ratio, inverse, sshare = factors(sabove, shere, sshare)
        ratio_side[level] = ratio
        g = (side_raw[level] + sabove * spartial) * inverse
        us[level, pl.ds(8, 24), :] = g
        return here, share, tuple(new), shere, sshare, g

    zero8 = jnp.zeros((8, CY), F32)
    zero24 = jnp.zeros((24, CY), F32)
    above, share, partial, sabove, sshare, spartial = lax.fori_loop(
        0, last_level, forward_rim,
        (zero8, zero8 + 1.0, (zero8,) * (TR + 1), zero24, zero24 + 1.0, zero24),
    )
    _, inverse, _ = factors(above, kv_halo[last_level], share)
    below = []
    for j in range(TR + 1):
        source = jnp.where(
            sub8 < 4, kv_halo[LEV + max(j - 1, 0)], kv_halo[LEV + min(j, TR - 1)]
        )
        x = (halo[last_level, pl.ds(8 * j, 8), :] + source + above * partial[j]) * inverse
        ue[last_level, pl.ds(STRIDE * j, 8), :] = x
        below.append(x)
    _, inverse, _ = factors(sabove, side_kv[last_level], sshare)
    sbelow = (side_raw[last_level] + side_flux + sabove * spartial) * inverse
    us[last_level, pl.ds(8, 24), :] = sbelow
    us[last_level, pl.ds(0, 8), :] = sbelow[16:24]

    def backward_rim(step, carry):
        level = last_level - 1 - step
        below, sbelow = carry
        ratio = ratio_halo[level]
        new = []
        for j in range(TR + 1):
            rows_j = pl.ds(STRIDE * j, 8)
            x = ue[level, rows_j, :] + ratio * below[j]
            ue[level, rows_j, :] = x
            new.append(x)
        x = us[level, pl.ds(8, 24), :] + ratio_side[level] * sbelow
        us[level, pl.ds(8, 24), :] = x
        us[level, pl.ds(0, 8), :] = x[16:24]
        return tuple(new), x

    lax.fori_loop(0, last_level, backward_rim, (tuple(below), sbelow))

    for copy in rows + edges + kvrows + kvedges:
        copy.wait_send()
    pltpu.make_async_copy(req.at[pl.ds(0, DEV - 1)], req.at[pl.ds(0, DEV - 1)], req_s).wait()
    pltpu.make_async_copy(rep.at[pl.ds(0, DEV - 1)], rep.at[pl.ds(0, DEV - 1)], rep_s).wait()


def smooth_kernel(ue, us, out, parts, weights, side_weights, side_out):
    block, blocks = pl.program_id(0), pl.num_programs(0)
    count = out.shape[1]
    held = count * CX
    lane = iota((held, CY), 1)

    def sides(at, into):
        levels = pl.ds(at * count, count)

        def cells(first):
            return us[levels, pl.ds(first, CX), :].reshape(held, CY)

        u = cells(8)
        q = 2.0 * (cells(7) + cells(9)) - 8.0 * u
        across = jnp.where(
            lane < 16,
            jnp.where(lane % 2 == 1, pltpu.roll(q, 1, 1), 0.0),
            jnp.where(lane % 2 == 0, pltpu.roll(q, CY - 1, 1), 0.0),
        )
        side = u + across
        rest = side - side.astype(BF16).astype(F32)
        both = jnp.where(lane < 32, side, jnp.where(lane < 64, pltpu.roll(rest, 32, 1), 0.0))
        side_out[into] = jnp.dot(both.astype(BF16), side_weights[...], preferred_element_type=F32)

    @pl.when(block == 0)
    def _():
        gap = jnp.abs(iota((CY, CY), 0) - iota((CY, CY), 1))
        first = jnp.where(gap == 0, 20.0, jnp.where(gap == 1, -8.0, jnp.where(gap == 2, 1.0, 0.0)))
        second = jnp.where(gap == 0, -8.0, jnp.where(gap == 1, 2.0, 0.0))
        for n, part in enumerate((first, first, second, second)):
            weights[pl.ds(n * CY, CY), :] = part.astype(BF16)
        row, col = iota((CY, CY), 0), iota((CY, CY), 1)
        goal = (row % 32) // 16 * 2 + row % 2
        for t in range(TR):
            hit = (row < 64) & ((row % 16) // 2 == t) & (col == (goal + CY - 2) % CY)
            side_weights[:, pl.ds(t * CY, CY)] = jnp.where(hit, 1.0, 0.0).astype(BF16)
        sides(0, 0)

    side_now = block % 2
    for n in range(count):
        level = block * count + n
        for t in range(TR):
            row = STRIDE * t + 8
            u = ue[level, pl.ds(row, CX), :]
            near = ue[level, pl.ds(row - 1, CX), :] + ue[level, pl.ds(row + 1, CX), :]
            for m, part in enumerate(split2(u) + split2(near)):
                parts[pl.ds((n * TR + t) * CX, CX), pl.ds(m * CY, CY)] = part
    mixed = jnp.dot(parts[...], weights[...], preferred_element_type=F32)
    for n in range(count):
        level = block * count + n
        for t in range(TR):
            row = STRIDE * t + 8
            u = ue[level, pl.ds(row, CX), :]
            far = ue[level, pl.ds(row - 2, CX), :] + ue[level, pl.ds(row + 2, CX), :]
            edge = side_out[side_now, pl.ds(n * CX, CX), pl.ds(t * CY, CY)]
            at = (n * TR + t) * CX
            out[t, n] = u - 0.025 * (far + edge + mixed[at : at + CX])
    sides(jnp.minimum(block + 1, blocks - 1), 1 - side_now)


def local(tracers, group_dest, group_slot, diffusivity, surface_flux):
    any_spec = pl.BlockSpec(memory_space=pltpu.HBM)
    dma = pltpu.SemaphoreType.DMA
    ue, us = pl.pallas_call(
        exchange_kernel,
        out_shape=(
            pltpu.VMEM((LEV, UROWS, CY), F32),
            pltpu.VMEM((LEV, 32, CY), F32),
        ),
        in_specs=[any_spec] * 5,
        out_specs=(pl.BlockSpec(memory_space=pltpu.VMEM), pl.BlockSpec(memory_space=pltpu.VMEM)),
        scratch_shapes=[
            pltpu.VMEM((TR, LEV, CX, CY), F32),
            pltpu.VMEM((CX, CY), jnp.int32),
            pltpu.VMEM((CX, CY), jnp.int32),
            pltpu.VMEM((VALS, SLOTS), F32),
            pltpu.VMEM((SLOTS, 256), BF16),
            pltpu.VMEM((CAP * DEV, SLOTS), BF16),
            pltpu.VMEM((SLOTS, 256), BF16),
            pltpu.VMEM((CX, CY), F32),
            pltpu.VMEM((DEV, SLOTS), BF16),
            pltpu.VMEM((16, SLOTS), BF16),
            pltpu.VMEM((CAP * DEV, SLOTS), BF16),
            pltpu.VMEM((DEV, 2 * CAP * CY), BF16),
            pltpu.VMEM((DEV, 1, CY), F32),
            pltpu.VMEM((DEV, 1, CY), F32),
            pltpu.VMEM((DEV, 4, CY), F32),
            pltpu.VMEM((DEV, 4, CY), F32),
            pltpu.VMEM((2 * VALS, CAP * DEV), BF16),
            pltpu.VMEM((VALS, SLOTS), F32),
            pltpu.VMEM((VALS, CX, CY), F32),
            pltpu.VMEM((3, CX, CY), F32),
            pltpu.VMEM((6, 3, CX, CY), F32),
            pltpu.VMEM((VALS, 8, CY), F32),
            pltpu.VMEM((LEV, 8 * (TR + 1), CY), F32),
            pltpu.VMEM((2, 9, CX, CY), F32),
            pltpu.VMEM((6, 9, CX, CY), F32),
            pltpu.VMEM((LEV, 24, CY), F32),
            pltpu.VMEM((LEV, 24, CY), F32),
            pltpu.VMEM((3, 24, CY), F32),
            pltpu.VMEM((LEV, CX, CY), F32),
            pltpu.VMEM((LEV, 8, CY), F32),
            pltpu.VMEM((LEV, 24, CY), F32),
            dma((4,)), dma, dma, dma, dma, dma,
            dma((2 * TR,)), dma((2 * TR,)), dma((6,)), dma((6,)),
            dma((2,)), dma((2,)), dma((6,)), dma((6,)),
        ],
        compiler_params=pltpu.CompilerParams(
            collective_id=0, has_side_effects=True, vmem_limit_bytes=44 << 20
        ),
        name="exchange",
    )(
        *(
            pltpu.with_memory_space_constraint(x, pltpu.HBM)
            for x in (tracers, group_dest, group_slot, diffusivity, surface_flux)
        )
    )
    count = 9
    whole = pl.BlockSpec(memory_space=pltpu.VMEM)
    return pl.pallas_call(
        smooth_kernel,
        grid=(LEV // count,),
        out_shape=jax.ShapeDtypeStruct(tracers.shape, F32),
        in_specs=[whole, whole],
        out_specs=pl.BlockSpec((TR, count, CX, CY), lambda b: (0, b, 0, 0)),
        scratch_shapes=[
            pltpu.VMEM((count * TR * CX, 4 * CY), BF16),
            pltpu.VMEM((4 * CY, CY), BF16),
            pltpu.VMEM((CY, TR * CY), BF16),
            pltpu.VMEM((2, count * CX, TR * CY), F32),
        ],
        compiler_params=pltpu.CompilerParams(vmem_limit_bytes=20 << 20),
        name="smooth",
    )(ue, us)


def solution(mesh):
    placed = (
        P(None, None, "fx", "fy"),
        P("fx", "fy"),
        P("fx", "fy"),
        P(None, ("fx", "fy")),
        P(None, ("fx", "fy")),
    )
    return jax.shard_map(
        local, mesh=mesh, in_specs=placed, out_specs=P(None, None, "fx", "fy"), check_vma=False
    )
```

```python
import jax
import jax.numpy as jnp
from jax import lax
from jax.experimental import pallas as pl
from jax.experimental.pallas import tpu as pltpu
from jax.sharding import PartitionSpec as P

MESH = pl.DeviceIdType.MESH
F32 = jnp.float32
BF16 = jnp.bfloat16
CAP = 6
N_FX, N_FY, DEV = 8, 16, 128
TR, LEV, CX, CY = 8, 72, 16, 128
SLOTS = 2048
VALS = LEV + TR
STRIDE = 24
UROWS = TR * STRIDE + 8


def iota(shape, dim):
    return lax.broadcasted_iota(jnp.int32, shape, dim)


def split2(x):
    hi = x.astype(BF16)
    lo = (x - hi.astype(F32)).astype(BF16)
    return hi, lo


def split3(x):
    hi = x.astype(BF16)
    rest = x - hi.astype(F32)
    mid = rest.astype(BF16)
    lo = (rest - mid.astype(F32)).astype(BF16)
    return hi, mid, lo


HOPS = (0, 1, 2, 1)
STEPS = sorted(
    (
        (dz, dx, dy, dc)
        for dz in range(4) for dx in range(4) for dy in range(4) for dc in range(2)
        if dz or dx or dy or dc
    ),
    key=lambda d: -(HOPS[d[0]] + HOPS[d[1]] + HOPS[d[2]]),
)


def all_peers(fx, fy):
    z, core, x, y = fx // 2, fx % 2, fy // 4, fy % 4
    zs, cores = [(z + d) % 4 * 2 for d in range(4)], [core, 1 - core]
    xs, ys = [(x + d) % 4 * 4 for d in range(4)], [(y + d) % 4 for d in range(4)]
    on_fx = {(dz, dc): zs[dz] + cores[dc] for dz in range(4) for dc in range(2)}
    on_fy = {(dx, dy): xs[dx] + ys[dy] for dx in range(4) for dy in range(4)}
    return [(on_fx[dz, dc], on_fy[dx, dy]) for dz, dx, dy, dc in STEPS]


def exchange_kernel(
    tracers, dest, slot, diff, flux,
    ue, us, ua, ub,
    tv, dest_v, slot_v, table, table_t, onehot, onehot_own, rank_v,
    matches, picks, chosen, widen, req, req_in, rep, rep_in, dsplit, kv_own, kv, edge_kv, edge_kv_in, kv_halo,
    halo, edge, edge_in, side_raw, side_kv, edge_kv_all, ratio_own, ratio_halo, ratio_side, parts, weights,
    load_sem, tv_sem, req_s, req_r, rep_s, rep_r, row_s, row_r, edge_s, edge_r,
    kvrow_s, kvrow_r, kvedge_s, kvedge_r,
):
    fx, fy = lax.axis_index("fx"), lax.axis_index("fy")
    me = fx * N_FY + fy
    up, down = (fx + N_FX - 1) % N_FX, (fx + 1) % N_FX
    left, right = (fy + N_FY - 1) % N_FY, (fy + 1) % N_FY

    loads = [
        pltpu.make_async_copy(dest, dest_v, load_sem.at[0]),
        pltpu.make_async_copy(slot, slot_v, load_sem.at[1]),
        pltpu.make_async_copy(diff, table.at[pl.ds(0, LEV)], load_sem.at[2]),
        pltpu.make_async_copy(flux, table.at[pl.ds(LEV, TR)], load_sem.at[3]),
    ]
    for load in loads:
        load.start()
    tv_load = pltpu.make_async_copy(tracers, tv, tv_sem)
    tv_load.start()

    barrier = pltpu.get_barrier_semaphore()
    peers = all_peers(fx, fy)

    def each_peer(action):
        for px, py in peers:
            action(px, py)

    def hello(px, py):
        pl.semaphore_signal(barrier, inc=1, device_id=(px, py), device_id_type=MESH)

    each_peer(hello)

    loads[0].wait()
    loads[1].wait()
    lane128 = iota((DEV, CY), 1)
    sub128 = iota((DEV, CY), 0)
    prefix = jnp.concatenate(
        [jnp.where(sub128 < lane128, 1.0, 0.0), jnp.ones((DEV, CY), F32)], 1
    ).astype(BF16)

    kk = iota((16, CY), 0)
    seen = jnp.zeros((DEV, CY), F32)
    for i in range(CX):
        d = dest_v[pl.ds(i, 1), :]
        d = jnp.where(d == me, -1, d)
        slots = slot_v[pl.ds(i, 1), :]
        match = jnp.where(d == sub128, 1.0, 0.0)
        mb = match.astype(BF16)
        matches[:, pl.ds(i * CY, CY)] = mb
        counts = jnp.dot(mb, prefix, preferred_element_type=F32)
        rank = jnp.sum(match * (counts[:, :CY] + seen), axis=0, keepdims=True)
        seen = seen + counts[:, CY:]
        rank_v[pl.ds(i, 1), :] = rank
        value = jnp.where(kk < 8, (slots >> 7) + 1, slots & 127).astype(F32)
        picks[:, pl.ds(i * CY, CY)] = jnp.where((kk & 7).astype(F32) == rank, value, 0.0).astype(BF16)
    asked = lax.dot_general(
        matches[...], picks[...], (((1,), (1,)), ((), ())), preferred_element_type=F32
    )
    req[:, 0, :] = jnp.concatenate([asked, jnp.zeros((DEV, CY - 16), F32)], 1)

    loads[2].wait()
    loads[3].wait()

    def flip(b, carry):
        cols = pl.ds(pl.multiple_of(b * 128, 128), 128)
        part = jnp.concatenate([table[:, cols], jnp.zeros((128 - VALS, 128), F32)], 0)
        hi, lo = split2(part.T)
        table_t[cols, pl.ds(0, 128)] = hi
        table_t[cols, pl.ds(128, 128)] = lo
        return carry

    lax.fori_loop(0, SLOTS // 128, flip, 0)

    for m in range(2 * CAP):
        lane_of = m if m < CAP else 8 + m - CAP
        widen[:, pl.ds(m * CY, CY)] = jnp.where(sub128 == lane_of, 1.0, 0.0).astype(BF16)

    def spread(i, carry):
        cols = pl.ds(pl.multiple_of(i * CY, CY), CY)
        d = dest_v[pl.ds(i, 1), :]
        d = jnp.where(d == me, -1, d)
        rank = rank_v[pl.ds(i, 1), :]
        hit = d == sub128
        for k in range(CAP):
            onehot[pl.ds(k * DEV, DEV), cols] = jnp.where(
                hit & (rank == float(k)), 1.0, 0.0
            ).astype(BF16)
        return carry

    lax.fori_loop(0, CX, spread, 0)
    pl.semaphore_wait(barrier, DEV - 1)

    def ask(px, py):
        pltpu.make_async_remote_copy(
            req.at[px * N_FY + py], req_in.at[me], req_s, req_r,
            device_id=(px, py), device_id_type=MESH,
        ).start()

    each_peer(ask)
    req_in[me] = jnp.zeros((1, CY), F32)

    rows = []
    for t in range(TR):
        rows.append(
            pltpu.make_async_remote_copy(
                tracers.at[t, :, pl.ds(14, 2), :],
                halo.at[:, pl.ds(8 * t + 6, 2), :],
                row_s.at[t], row_r.at[t], device_id=(down, fy), device_id_type=MESH,
            )
        )
        rows.append(
            pltpu.make_async_remote_copy(
                tracers.at[t, :, pl.ds(0, 2), :],
                halo.at[:, pl.ds(8 * t + 8, 2), :],
                row_s.at[TR + t], row_r.at[TR + t], device_id=(up, fy), device_id_type=MESH,
            )
        )
    for copy in rows:
        copy.start()

    tv_load.wait()
    lane16 = iota((CX, CY), 1)

    def pack(q, carry):
        first = last = jnp.zeros((CX, CY), F32)
        for lg in range(8):
            for t in range(TR):
                cells = tv[t, q + 9 * lg]
                at = 16 * lg + 2 * t
                here = (lane16 == at) | (lane16 == at + 1)
                first = jnp.where(here, pltpu.roll(cells, at, 1) if at else cells, first)
                moved = pltpu.roll(cells, (at + 2) % 128, 1) if (at + 2) % 128 else cells
                last = jnp.where(here, moved, last)
        edge[0, q] = last
        edge[1, q] = first
        return carry

    lax.fori_loop(0, 9, pack, 0)

    def to_sides(sources, target, sends, receives):
        places = [
            (fx, right, 0, 0, CX), (fx, left, 1, 0, CX),
            (down, right, 2, CX - 1, 1), (down, left, 3, CX - 1, 1),
            (up, right, 4, 0, 1), (up, left, 5, 0, 1),
        ]
        copies = [
            pltpu.make_async_remote_copy(
                sources[n % 2].at[:, pl.ds(first, count), :],
                target.at[n, :, pl.ds(first, count), :],
                sends.at[n], receives.at[n], device_id=(px, py), device_id_type=MESH,
            )
            for px, py, n, first, count in places
        ]
        for copy in copies:
            copy.start()
        return copies

    edges = to_sides((edge.at[0], edge.at[1]), edge_in, edge_s, edge_r)

    gap = jnp.abs(sub128 - lane128)
    first = jnp.where(gap == 0, 20.0, jnp.where(gap == 1, -8.0, jnp.where(gap == 2, 1.0, 0.0)))
    second = jnp.where(gap == 0, -8.0, jnp.where(gap == 1, 2.0, 0.0))
    for n in range(2):
        weights[pl.ds(n * CY, CY), pl.ds(0, CY)] = first.astype(BF16)
        weights[pl.ds(n * CY, CY), pl.ds(CY, CY)] = second.astype(BF16)

    pltpu.make_async_copy(req_in.at[pl.ds(0, DEV - 1)], req_in.at[pl.ds(0, DEV - 1)], req_r).wait()
    wanted = req_in[:, 0, :]
    zero_b = jnp.zeros((DEV, CY), BF16)
    zero_f = jnp.zeros((DEV, CY), F32)
    lane_f = lane128.astype(F32)
    apart = jnp.dot(wanted.astype(BF16), widen[...], preferred_element_type=F32)
    for k in range(CAP):
        high = apart[:, k * CY : (k + 1) * CY].astype(BF16)
        low = jnp.where(apart[:, (CAP + k) * CY : (CAP + k + 1) * CY] == lane_f, 1.0, 0.0).astype(BF16)
        for b in range(SLOTS // 128):
            chosen[pl.ds(k * DEV, DEV), pl.ds(b * 128, 128)] = jnp.where(high == float(b + 1), low, zero_b)
    both = jnp.dot(chosen[...], table_t[...], preferred_element_type=F32)
    both = both[:, :128] + both[:, 128:]
    got = [both[k * DEV : (k + 1) * DEV] for k in range(CAP)]
    for j in range(3):
        rep[:, j, :] = jnp.where(lane128 < 64, got[2 * j], pltpu.roll(got[2 * j + 1], 64, 1))
    tail = jnp.zeros((DEV, CY), F32)
    for k in range(CAP):
        shift = (16 * k - 64) % 128
        moved = pltpu.roll(got[k], shift, 1) if shift else got[k]
        tail = jnp.where(lane128 // 16 == k, moved, tail)
    rep[:, 3, :] = tail

    def answer(px, py):
        pltpu.make_async_remote_copy(
            rep.at[px * N_FY + py], rep_in.at[me], rep_s, rep_r,
            device_id=(px, py), device_id_type=MESH,
        ).start()

    each_peer(answer)
    rep_in[me] = jnp.zeros((4, CY), F32)

    tab3 = jnp.concatenate(split3(table[...]), 0)

    def keep(i, carry):
        for half in range(2):
            d = dest_v[pl.ds(2 * i + half, 1), :]
            s = jnp.where(d == me, slot_v[pl.ds(2 * i + half, 1), :], -1)
            high = ((s >> 7).astype(F32) + zero_f).astype(BF16)
            low = jnp.where((s & 127) == sub128, 1.0, 0.0).astype(BF16)
            for b in range(SLOTS // 128):
                onehot_own[pl.ds(b * 128, 128), pl.ds(half * CY, CY)] = jnp.where(
                    high == float(b), low, zero_b
                )
        three = jnp.dot(tab3, onehot_own[...], preferred_element_type=F32)
        kv_own[:, pl.ds(pl.multiple_of(i * 2 * CY, 2 * CY), 2 * CY)] = (
            three[:VALS] + three[VALS : 2 * VALS] + three[2 * VALS :]
        )
        return carry

    lax.fori_loop(0, CX // 2, keep, 0)

    for copy in edges:
        copy.wait_recv()
    lane8 = iota((8, CY), 1)
    sub8 = iota((8, CY), 0)
    lane24 = iota((24, CY), 1)

    def gather_edges(q, carry):
        def merged(n, rows):
            return edge_in[n + 1, q, rows], edge_in[n, q, rows]

        sides = merged(0, pl.ds(0, CX))
        over = merged(2, pl.ds(8, 8))
        under = merged(4, pl.ds(0, 8))
        right_cells, left_cells = (
            jnp.concatenate([a, jnp.where(sub8 == 7, b, c)], 0)
            for a, b, c in zip(sides, over, under)
        )
        for lg in range(8):
            near_r = pltpu.roll(right_cells, 128 - 16 * lg, 1) if lg else right_cells
            near_l = pltpu.roll(left_cells, (144 - 16 * lg) % 128, 1) if lg != 1 else left_cells
            side_raw[9 * lg + q] = jnp.where(lane24 < 16, near_r, near_l)
        return carry

    lax.fori_loop(0, 9, gather_edges, 0)

    pltpu.make_async_copy(rep_in.at[pl.ds(0, DEV - 1)], rep_in.at[pl.ds(0, DEV - 1)], rep_r).wait()
    last = rep_in[:, 3, :]
    for k in range(CAP):
        main = rep_in[:, k // 2, :]
        if k % 2:
            main = pltpu.roll(main, 64, 1)
        shift = (64 - 16 * k) % 128
        end = pltpu.roll(last, shift, 1) if shift else last
        cols = jnp.where(lane128 < 64, main, jnp.where(lane128 < VALS, end, 0.0))
        hi, lo = split2(cols.T[:VALS])
        dsplit[pl.ds(0, VALS), pl.ds(k * DEV, DEV)] = hi
        dsplit[pl.ds(VALS, VALS), pl.ds(k * DEV, DEV)] = lo

    def assemble(i, carry):
        cols = pl.ds(pl.multiple_of(i * 2 * CY, 2 * CY), 2 * CY)
        two = jnp.dot(dsplit[...], onehot[:, cols], preferred_element_type=F32)
        full = kv_own[:, cols] + two[:VALS] + two[VALS:]
        kv[:, 2 * i, :] = full[:, :CY]
        kv[:, 2 * i + 1, :] = full[:, CY:]
        return carry

    for i in range(CX // 2):
        assemble(i, 0)

    kvrows = [
        pltpu.make_async_remote_copy(
            kv.at[:, pl.ds(14, 2), :], kv_halo.at[:, pl.ds(6, 2), :],
            kvrow_s.at[0], kvrow_r.at[0], device_id=(down, fy), device_id_type=MESH,
        ),
        pltpu.make_async_remote_copy(
            kv.at[:, pl.ds(0, 2), :], kv_halo.at[:, pl.ds(0, 2), :],
            kvrow_s.at[1], kvrow_r.at[1], device_id=(up, fy), device_id_type=MESH,
        ),
    ]
    for copy in kvrows:
        copy.start()
    for g in range(3):
        acc = jnp.zeros((CX, CY), F32)
        for m in range(32 if g < 2 else VALS - 64):
            moved = pltpu.roll(kv[32 * g + m], 4 * m + 2, 1) if 4 * m + 2 < 128 else kv[32 * g + m]
            acc = jnp.where(lane16 // 4 == m, moved, acc)
        edge_kv[g] = acc
    kvedges = to_sides((edge_kv, edge_kv), edge_kv_in, kvedge_s, kvedge_r)

    def factors(before, after, share):
        rest = 1.0 + before * share
        inverse = 1.0 / (rest + after)
        return after * inverse, inverse, rest * inverse

    def solve(*systems):
        def inwards(step, carry):
            done = []
            for (coupling, ratios, right_sides, count, put, _), state in zip(systems, carry):
                for (before, share, partial), level, nearer in zip(
                    state, (step, LEV - 1 - step), (step, LEV - 2 - step)
                ):
                    after = coupling[nearer]
                    ratio, inverse, share = factors(before, after, share)
                    ratios[level] = ratio
                    new = []
                    for j in range(count):
                        g = (right_sides(level, j) + before * partial[j]) * inverse
                        put(level, j, g)
                        new.append(g)
                    done.append((after, share, tuple(new)))
            return tuple(zip(done[0::2], done[1::2]))

        start = []
        for coupling, _, _, count, _, _ in systems:
            last = coupling[LEV - 1]
            zero = jnp.zeros_like(last)
            zeros = (zero,) * count
            start.append(((zero, zero + 1.0, zeros), (last, zero + 1.0, zeros)))
        met = lax.fori_loop(0, LEV // 2, inwards, tuple(start))
        high, low = LEV // 2 - 1, LEV // 2
        ends = []
        for (_, ratios, _, count, put, _), ((_, _, top), (_, _, bottom)) in zip(systems, met):
            e, f = ratios[high], ratios[low]
            scale = 1.0 / (1.0 - e * f)
            above, below = [], []
            for j in range(count):
                x = (top[j] + e * bottom[j]) * scale
                y = bottom[j] + f * x
                put(high, j, x)
                put(low, j, y)
                above.append(x)
                below.append(y)
            ends.append((tuple(above), tuple(below)))

        def outwards(step, carry):
            done = []
            for (_, ratios, _, count, put, get), state in zip(systems, carry):
                for last, level in zip(state, (high - 1 - step, low + 1 + step)):
                    ratio = ratios[level]
                    new = []
                    for j in range(count):
                        x = get(level, j) + ratio * last[j]
                        put(level, j, x)
                        new.append(x)
                    done.append(tuple(new))
            return tuple(zip(done[0::2], done[1::2]))

        lax.fori_loop(0, LEV // 2 - 1, outwards, tuple(ends))

    for t in range(TR):
        tv[t, LEV - 1] = tv[t, LEV - 1] + kv[LEV + t]

    def put_own(level, t, x):
        ue[level, pl.ds(STRIDE * t + 8, CX), :] = x

    solve(
        (kv, ratio_own, lambda level, t: tv[t, level], TR, put_own,
         lambda level, t: ue[level, pl.ds(STRIDE * t + 8, CX), :])
    )

    def mix(b, carry):
        group = 9
        for n in range(group):
            for t in range(TR):
                at = pl.ds((n * TR + t) * CX, CX)
                hi, lo = split2(ue[b * group + n, pl.ds(STRIDE * t + 8, CX), :])
                parts[at, pl.ds(0, CY)] = hi
                parts[at, pl.ds(CY, CY)] = lo
        mixed = jnp.dot(parts[...], weights[...], preferred_element_type=F32)
        for n in range(group):
            for t in range(TR):
                own = pl.ds(STRIDE * t + 8, CX)
                at = (n * TR + t) * CX
                both = mixed[at : at + CX]
                ua[b * group + n, pl.ds(t * CX, CX), :] = (
                    ue[b * group + n, own, :] - 0.025 * both[:, :CY]
                )
                ub[b * group + n, own, :] = both[:, CY:]
        return carry

    lax.fori_loop(0, LEV // 9, mix, 0)

    for copy in kvrows + kvedges:
        copy.wait_recv()
    for copy in rows:
        copy.wait_recv()
    for g in range(3):
        edge_kv_all[g, pl.ds(0, CX), :] = jnp.where(lane16 % 4 < 2, edge_kv_in[0, g], edge_kv_in[1, g])
        over = jnp.where(lane8 % 4 < 2, edge_kv_in[2, g, pl.ds(8, 8)], edge_kv_in[3, g, pl.ds(8, 8)])
        under = jnp.where(lane8 % 4 < 2, edge_kv_in[4, g, pl.ds(0, 8)], edge_kv_in[5, g, pl.ds(0, 8)])
        edge_kv_all[g, pl.ds(CX, 8), :] = jnp.where(sub8 == 7, over, under)
    quad = jnp.where(lane24 % 32 < 16, 2, 0) + lane24 % 2

    for level in range(LEV):
        side_kv[level] = jnp.take_along_axis(
            edge_kv_all[level // 32], 4 * (level % 32) + quad, axis=1
        )

    side_flux = jnp.take_along_axis(
        edge_kv_all[2], 32 + 4 * ((lane24 % 16) // 2) + quad, axis=1
    )

    for j in range(TR + 1):
        tile = pl.ds(8 * j, 8)
        halo[LEV - 1, tile, :] = halo[LEV - 1, tile, :] + jnp.where(
            sub8 < 4, kv_halo[LEV + max(j - 1, 0)], kv_halo[LEV + min(j, TR - 1)]
        )
    side_raw[LEV - 1] = side_raw[LEV - 1] + side_flux

    def put_rows(level, j, x):
        ue[level, pl.ds(STRIDE * j, 8), :] = x

    def put_side(level, j, x):
        us[level, pl.ds(8, 24), :] = x
        us[level, pl.ds(0, 8), :] = x[CX:]

    solve(
        (kv_halo, ratio_halo, lambda level, j: halo[level, pl.ds(8 * j, 8), :], TR + 1, put_rows,
         lambda level, j: ue[level, pl.ds(STRIDE * j, 8), :]),
        (side_kv, ratio_side, lambda level, j: side_raw[level], 1, put_side,
         lambda level, j: us[level, pl.ds(8, 24), :]),
    )

    for level in range(LEV):
        rim = jnp.concatenate(
            [ue[level, pl.ds(7, TR, stride=STRIDE), :], ue[level, pl.ds(STRIDE, TR, stride=STRIDE), :]], 0
        )
        hi, lo = split2(rim)
        parts[pl.ds(level * 2 * TR, 2 * TR), pl.ds(0, CY)] = hi
        parts[pl.ds(level * 2 * TR, 2 * TR), pl.ds(CY, CY)] = lo
    fixed = jnp.dot(parts[...], weights[:, pl.ds(CY, CY)], preferred_element_type=F32)
    for level in range(LEV):
        at = level * 2 * TR
        ub[level, pl.ds(7, TR, stride=STRIDE), :] = fixed[at : at + TR]
        ub[level, pl.ds(STRIDE, TR, stride=STRIDE), :] = fixed[at + TR : at + 2 * TR]

    for copy in rows + edges + kvrows + kvedges:
        copy.wait_send()
    pltpu.make_async_copy(req.at[pl.ds(0, DEV - 1)], req.at[pl.ds(0, DEV - 1)], req_s).wait()
    pltpu.make_async_copy(rep.at[pl.ds(0, DEV - 1)], rep.at[pl.ds(0, DEV - 1)], rep_s).wait()


def smooth_kernel(ue, us, ua, ub, out, held, side_weights, side_out, sem):
    row, col = iota((CY, CY), 0), iota((CY, CY), 1)
    goal = (row % 32) // 16 * 2 + row % 2
    for t in range(TR):
        hit = (row < 64) & ((row % 16) // 2 == t) & (col == (goal + CY - 2) % CY)
        side_weights[:, pl.ds(t * CY, CY)] = jnp.where(hit, 1.0, 0.0).astype(BF16)

    def cells(first):
        return us[:, pl.ds(first, CX), :].reshape(LEV * CX, CY)

    lane = iota((LEV * CX, CY), 1)
    u = cells(8)
    q = 2.0 * (cells(7) + cells(9)) - 8.0 * u
    across = jnp.where(
        lane < 16,
        jnp.where(lane % 2 == 1, pltpu.roll(q, 1, 1), 0.0),
        jnp.where(lane % 2 == 0, pltpu.roll(q, CY - 1, 1), 0.0),
    )
    side = u + across
    rest = side - side.astype(BF16).astype(F32)
    both = jnp.where(lane < 32, side, jnp.where(lane < 64, pltpu.roll(rest, 32, 1), 0.0))
    side_out[...] = jnp.dot(both.astype(BF16), side_weights[...], preferred_element_type=F32)

    count = 9
    copies = []
    for block in range(LEV // count):
        for level in range(block * count, (block + 1) * count):
            for t in range(TR):
                row = STRIDE * t + 8
                near = ub[level, pl.ds(row - 1, CX), :] + ub[level, pl.ds(row + 1, CX), :]
                far = ue[level, pl.ds(row - 2, CX), :] + ue[level, pl.ds(row + 2, CX), :]
                edge = side_out[pl.ds(level * CX, CX), pl.ds(t * CY, CY)]
                held[t, level] = ua[level, pl.ds(t * CX, CX), :] - 0.025 * ((far + near) + edge)
        levels = pl.ds(block * count, count)
        copy = pltpu.make_async_copy(held.at[:, levels], out.at[:, levels], sem.at[block])
        copy.start()
        copies.append(copy)
    for copy in copies:
        copy.wait()


def local(tracers, group_dest, group_slot, diffusivity, surface_flux):
    any_spec = pl.BlockSpec(memory_space=pltpu.HBM)
    dma = pltpu.SemaphoreType.DMA
    ue, us, ua, ub = pl.pallas_call(
        exchange_kernel,
        out_shape=(
            pltpu.VMEM((LEV, UROWS, CY), F32),
            pltpu.VMEM((LEV, 32, CY), F32),
            pltpu.VMEM((LEV, TR * CX, CY), F32),
            pltpu.VMEM((LEV, UROWS, CY), F32),
        ),
        in_specs=[any_spec] * 5,
        out_specs=(pl.BlockSpec(memory_space=pltpu.VMEM),) * 4,
        scratch_shapes=[
            pltpu.VMEM((TR, LEV, CX, CY), F32),
            pltpu.VMEM((CX, CY), jnp.int32),
            pltpu.VMEM((CX, CY), jnp.int32),
            pltpu.VMEM((VALS, SLOTS), F32),
            pltpu.VMEM((SLOTS, 256), BF16),
            pltpu.VMEM((CAP * DEV, SLOTS), BF16),
            pltpu.VMEM((SLOTS, 256), BF16),
            pltpu.VMEM((CX, CY), F32),
            pltpu.VMEM((DEV, SLOTS), BF16),
            pltpu.VMEM((16, SLOTS), BF16),
            pltpu.VMEM((CAP * DEV, SLOTS), BF16),
            pltpu.VMEM((DEV, 2 * CAP * CY), BF16),
            pltpu.VMEM((DEV, 1, CY), F32),
            pltpu.VMEM((DEV, 1, CY), F32),
            pltpu.VMEM((DEV, 4, CY), F32),
            pltpu.VMEM((DEV, 4, CY), F32),
            pltpu.VMEM((2 * VALS, CAP * DEV), BF16),
            pltpu.VMEM((VALS, SLOTS), F32),
            pltpu.VMEM((VALS, CX, CY), F32),
            pltpu.VMEM((3, CX, CY), F32),
            pltpu.VMEM((6, 3, CX, CY), F32),
            pltpu.VMEM((VALS, 8, CY), F32),
            pltpu.VMEM((LEV, 8 * (TR + 1), CY), F32),
            pltpu.VMEM((2, 9, CX, CY), F32),
            pltpu.VMEM((6, 9, CX, CY), F32),
            pltpu.VMEM((LEV, 24, CY), F32),
            pltpu.VMEM((LEV, 24, CY), F32),
            pltpu.VMEM((3, 24, CY), F32),
            pltpu.VMEM((LEV, CX, CY), F32),
            pltpu.VMEM((LEV, 8, CY), F32),
            pltpu.VMEM((LEV, 24, CY), F32),
            pltpu.VMEM((9 * TR * CX, 2 * CY), BF16),
            pltpu.VMEM((2 * CY, 2 * CY), BF16),
            dma((4,)), dma, dma, dma, dma, dma,
            dma((2 * TR,)), dma((2 * TR,)), dma((6,)), dma((6,)),
            dma((2,)), dma((2,)), dma((6,)), dma((6,)),
        ],
        compiler_params=pltpu.CompilerParams(
            collective_id=0, has_side_effects=True, vmem_limit_bytes=30 << 20
        ),
        name="exchange",
    )(
        *(
            pltpu.with_memory_space_constraint(x, pltpu.HBM)
            for x in (tracers, group_dest, group_slot, diffusivity, surface_flux)
        )
    )
    whole = pl.BlockSpec(memory_space=pltpu.VMEM)
    return pl.pallas_call(
        smooth_kernel,
        out_shape=jax.ShapeDtypeStruct(tracers.shape, F32),
        in_specs=[whole] * 4,
        out_specs=pl.BlockSpec(memory_space=pl.ANY),
        scratch_shapes=[
            pltpu.VMEM((TR, LEV, CX, CY), F32),
            pltpu.VMEM((CY, TR * CY), BF16),
            pltpu.VMEM((LEV * CX, TR * CY), F32),
            dma((8,)),
        ],
        compiler_params=pltpu.CompilerParams(vmem_limit_bytes=16 << 20),
        name="smooth",
    )(ue, us, ua, ub)


def solution(mesh):
    placed = (
        P(None, None, "fx", "fy"),
        P("fx", "fy"),
        P("fx", "fy"),
        P(None, ("fx", "fy")),
        P(None, ("fx", "fy")),
    )
    return jax.shard_map(
        local, mesh=mesh, in_specs=placed, out_specs=P(None, None, "fx", "fy"), check_vma=False
    )
```

```python
import jax
import jax.numpy as jnp
from jax import lax
from jax.experimental import pallas as pl
from jax.experimental.pallas import tpu as pltpu
from jax.sharding import PartitionSpec as P

MESH = pl.DeviceIdType.MESH
F32 = jnp.float32
BF16 = jnp.bfloat16
CAP = 6
N_FX, N_FY, DEV = 8, 16, 128
TR, LEV, CX, CY = 8, 72, 16, 128
SLOTS = 2048
VALS = LEV + TR
STRIDE = 24
UROWS = TR * STRIDE + 8


def iota(shape, dim):
    return lax.broadcasted_iota(jnp.int32, shape, dim)


def split2(x):
    hi = x.astype(BF16)
    lo = (x - hi.astype(F32)).astype(BF16)
    return hi, lo


def split3(x):
    hi = x.astype(BF16)
    rest = x - hi.astype(F32)
    mid = rest.astype(BF16)
    lo = (rest - mid.astype(F32)).astype(BF16)
    return hi, mid, lo


HOPS = (0, 1, 2, 1)
STEPS = sorted(
    (
        (dz, dx, dy, dc)
        for dz in range(4) for dx in range(4) for dy in range(4) for dc in range(2)
        if dz or dx or dy or dc
    ),
    key=lambda d: -(HOPS[d[0]] + HOPS[d[1]] + HOPS[d[2]]),
)


def all_peers(fx, fy):
    z, core, x, y = fx // 2, fx % 2, fy // 4, fy % 4
    zs, cores = [(z + d) % 4 * 2 for d in range(4)], [core, 1 - core]
    xs, ys = [(x + d) % 4 * 4 for d in range(4)], [(y + d) % 4 for d in range(4)]
    on_fx = {(dz, dc): zs[dz] + cores[dc] for dz in range(4) for dc in range(2)}
    on_fy = {(dx, dy): xs[dx] + ys[dy] for dx in range(4) for dy in range(4)}
    return [(on_fx[dz, dc], on_fy[dx, dy]) for dz, dx, dy, dc in STEPS]


def exchange_kernel(
    tracers, dest, slot, diff, flux,
    us, ua,
    ue, ub, tv, dest_v, slot_v, table, table_t, onehot, onehot_own, rank_v,
    matches, picks, chosen, widen, req, req_in, rep, rep_in, dsplit, kv_own, kv, edge_kv, edge_kv_in, kv_halo,
    halo, edge, edge_in, side_raw, side_kv, edge_kv_all, ratio_own, ratio_halo, ratio_side, parts, weights,
    load_sem, tv_sem, req_s, req_r, rep_s, rep_r, row_s, row_r, edge_s, edge_r,
    kvrow_s, kvrow_r, kvedge_s, kvedge_r,
):
    fx, fy = lax.axis_index("fx"), lax.axis_index("fy")
    me = fx * N_FY + fy
    up, down = (fx + N_FX - 1) % N_FX, (fx + 1) % N_FX
    left, right = (fy + N_FY - 1) % N_FY, (fy + 1) % N_FY

    loads = [
        pltpu.make_async_copy(dest, dest_v, load_sem.at[0]),
        pltpu.make_async_copy(slot, slot_v, load_sem.at[1]),
        pltpu.make_async_copy(diff, table.at[pl.ds(0, LEV)], load_sem.at[2]),
        pltpu.make_async_copy(flux, table.at[pl.ds(LEV, TR)], load_sem.at[3]),
    ]
    for load in loads:
        load.start()
    tv_load = pltpu.make_async_copy(tracers, tv, tv_sem)
    tv_load.start()

    barrier = pltpu.get_barrier_semaphore()
    peers = all_peers(fx, fy)

    def each_peer(action):
        for px, py in peers:
            action(px, py)

    def hello(px, py):
        pl.semaphore_signal(barrier, inc=1, device_id=(px, py), device_id_type=MESH)

    each_peer(hello)

    loads[0].wait()
    loads[1].wait()
    lane128 = iota((DEV, CY), 1)
    sub128 = iota((DEV, CY), 0)
    prefix = jnp.concatenate(
        [jnp.where(sub128 < lane128, 1.0, 0.0), jnp.ones((DEV, CY), F32)], 1
    ).astype(BF16)

    kk = iota((16, CY), 0)
    seen = jnp.zeros((DEV, CY), F32)
    for i in range(CX):
        d = dest_v[pl.ds(i, 1), :]
        d = jnp.where(d == me, -1, d)
        slots = slot_v[pl.ds(i, 1), :]
        match = jnp.where(d == sub128, 1.0, 0.0)
        mb = match.astype(BF16)
        matches[:, pl.ds(i * CY, CY)] = mb
        counts = jnp.dot(mb, prefix, preferred_element_type=F32)
        rank = jnp.sum(match * (counts[:, :CY] + seen), axis=0, keepdims=True)
        seen = seen + counts[:, CY:]
        rank_v[pl.ds(i, 1), :] = rank
        value = jnp.where(kk < 8, (slots >> 7) + 1, slots & 127).astype(F32)
        picks[:, pl.ds(i * CY, CY)] = jnp.where((kk & 7).astype(F32) == rank, value, 0.0).astype(BF16)
    asked = lax.dot_general(
        matches[...], picks[...], (((1,), (1,)), ((), ())), preferred_element_type=F32
    )
    req[:, 0, :] = jnp.concatenate([asked, jnp.zeros((DEV, CY - 16), F32)], 1)

    loads[2].wait()
    loads[3].wait()

    def flip(b, carry):
        cols = pl.ds(pl.multiple_of(b * 128, 128), 128)
        part = jnp.concatenate([table[:, cols], jnp.zeros((128 - VALS, 128), F32)], 0)
        hi, lo = split2(part.T)
        table_t[cols, pl.ds(0, 128)] = hi
        table_t[cols, pl.ds(128, 128)] = lo
        return carry

    lax.fori_loop(0, SLOTS // 128, flip, 0)

    for m in range(2 * CAP):
        lane_of = m if m < CAP else 8 + m - CAP
        widen[:, pl.ds(m * CY, CY)] = jnp.where(sub128 == lane_of, 1.0, 0.0).astype(BF16)

    def spread(i, carry):
        cols = pl.ds(pl.multiple_of(i * CY, CY), CY)
        d = dest_v[pl.ds(i, 1), :]
        d = jnp.where(d == me, -1, d)
        rank = rank_v[pl.ds(i, 1), :]
        hit = d == sub128
        for k in range(CAP):
            onehot[pl.ds(k * DEV, DEV), cols] = jnp.where(
                hit & (rank == float(k)), 1.0, 0.0
            ).astype(BF16)
        return carry

    lax.fori_loop(0, CX, spread, 0)
    pl.semaphore_wait(barrier, DEV - 1)

    def ask(px, py):
        pltpu.make_async_remote_copy(
            req.at[px * N_FY + py], req_in.at[me], req_s, req_r,
            device_id=(px, py), device_id_type=MESH,
        ).start()

    each_peer(ask)
    req_in[me] = jnp.zeros((1, CY), F32)

    rows = []
    for t in range(TR):
        rows.append(
            pltpu.make_async_remote_copy(
                tracers.at[t, :, pl.ds(14, 2), :],
                halo.at[:, pl.ds(8 * t + 6, 2), :],
                row_s.at[t], row_r.at[t], device_id=(down, fy), device_id_type=MESH,
            )
        )
        rows.append(
            pltpu.make_async_remote_copy(
                tracers.at[t, :, pl.ds(0, 2), :],
                halo.at[:, pl.ds(8 * t + 8, 2), :],
                row_s.at[TR + t], row_r.at[TR + t], device_id=(up, fy), device_id_type=MESH,
            )
        )
    for copy in rows:
        copy.start()

    tv_load.wait()
    lane16 = iota((CX, CY), 1)

    def pack(q, carry):
        first = last = jnp.zeros((CX, CY), F32)
        for lg in range(8):
            for t in range(TR):
                cells = tv[t, q + 9 * lg]
                at = 16 * lg + 2 * t
                here = (lane16 == at) | (lane16 == at + 1)
                first = jnp.where(here, pltpu.roll(cells, at, 1) if at else cells, first)
                moved = pltpu.roll(cells, (at + 2) % 128, 1) if (at + 2) % 128 else cells
                last = jnp.where(here, moved, last)
        edge[0, q] = last
        edge[1, q] = first
        return carry

    lax.fori_loop(0, 9, pack, 0)

    def to_sides(sources, target, sends, receives):
        places = [
            (fx, right, 0, 0, CX), (fx, left, 1, 0, CX),
            (down, right, 2, CX - 1, 1), (down, left, 3, CX - 1, 1),
            (up, right, 4, 0, 1), (up, left, 5, 0, 1),
        ]
        copies = [
            pltpu.make_async_remote_copy(
                sources[n % 2].at[:, pl.ds(first, count), :],
                target.at[n, :, pl.ds(first, count), :],
                sends.at[n], receives.at[n], device_id=(px, py), device_id_type=MESH,
            )
            for px, py, n, first, count in places
        ]
        for copy in copies[2:] + copies[:2]:
            copy.start()
        return copies

    edges = to_sides((edge.at[0], edge.at[1]), edge_in, edge_s, edge_r)

    gap = jnp.abs(sub128 - lane128)
    first = jnp.where(gap == 0, 20.0, jnp.where(gap == 1, -8.0, jnp.where(gap == 2, 1.0, 0.0)))
    second = jnp.where(gap == 0, -8.0, jnp.where(gap == 1, 2.0, 0.0))
    for n in range(2):
        weights[pl.ds(n * CY, CY), pl.ds(0, CY)] = first.astype(BF16)
        weights[pl.ds(n * CY, CY), pl.ds(CY, CY)] = second.astype(BF16)

    def clear(level, carry):
        for j in range(TR + 1):
            ue[level, pl.ds(STRIDE * j, 8), :] = jnp.zeros((8, CY), F32)
            ub[level, pl.ds(STRIDE * j, 8), :] = jnp.zeros((8, CY), F32)
        return carry

    lax.fori_loop(0, LEV, clear, 0)

    pltpu.make_async_copy(req_in.at[pl.ds(0, DEV - 1)], req_in.at[pl.ds(0, DEV - 1)], req_r).wait()
    wanted = req_in[:, 0, :]
    zero_b = jnp.zeros((DEV, CY), BF16)
    zero_f = jnp.zeros((DEV, CY), F32)
    lane_f = lane128.astype(F32)
    apart = jnp.dot(wanted.astype(BF16), widen[...], preferred_element_type=F32)
    for k in range(CAP):
        high = apart[:, k * CY : (k + 1) * CY].astype(BF16)
        low = jnp.where(apart[:, (CAP + k) * CY : (CAP + k + 1) * CY] == lane_f, 1.0, 0.0).astype(BF16)
        for b in range(SLOTS // 128):
            chosen[pl.ds(k * DEV, DEV), pl.ds(b * 128, 128)] = jnp.where(high == float(b + 1), low, zero_b)
    both = jnp.dot(chosen[...], table_t[...], preferred_element_type=F32)
    both = both[:, :128] + both[:, 128:]
    got = [both[k * DEV : (k + 1) * DEV] for k in range(CAP)]
    for j in range(3):
        rep[:, j, :] = jnp.where(lane128 < 64, got[2 * j], pltpu.roll(got[2 * j + 1], 64, 1))
    tail = jnp.zeros((DEV, CY), F32)
    for k in range(CAP):
        shift = (16 * k - 64) % 128
        moved = pltpu.roll(got[k], shift, 1) if shift else got[k]
        tail = jnp.where(lane128 // 16 == k, moved, tail)
    rep[:, 3, :] = tail

    def answer(px, py):
        pltpu.make_async_remote_copy(
            rep.at[px * N_FY + py], rep_in.at[me], rep_s, rep_r,
            device_id=(px, py), device_id_type=MESH,
        ).start()

    each_peer(answer)
    rep_in[me] = jnp.zeros((4, CY), F32)

    tab3 = jnp.concatenate(split3(table[...]), 0)

    def keep(i, carry):
        for half in range(2):
            d = dest_v[pl.ds(2 * i + half, 1), :]
            s = jnp.where(d == me, slot_v[pl.ds(2 * i + half, 1), :], -1)
            high = ((s >> 7).astype(F32) + zero_f).astype(BF16)
            low = jnp.where((s & 127) == sub128, 1.0, 0.0).astype(BF16)
            for b in range(SLOTS // 128):
                onehot_own[pl.ds(b * 128, 128), pl.ds(half * CY, CY)] = jnp.where(
                    high == float(b), low, zero_b
                )
        three = jnp.dot(tab3, onehot_own[...], preferred_element_type=F32)
        kv_own[:, pl.ds(pl.multiple_of(i * 2 * CY, 2 * CY), 2 * CY)] = (
            three[:VALS] + three[VALS : 2 * VALS] + three[2 * VALS :]
        )
        return carry

    lax.fori_loop(0, CX // 2, keep, 0)

    for copy in edges:
        copy.wait_recv()
    lane8 = iota((8, CY), 1)
    sub8 = iota((8, CY), 0)
    lane24 = iota((24, CY), 1)

    def gather_edges(q, carry):
        def merged(n, rows):
            return edge_in[n + 1, q, rows], edge_in[n, q, rows]

        sides = merged(0, pl.ds(0, CX))
        over = merged(2, pl.ds(8, 8))
        under = merged(4, pl.ds(0, 8))
        right_cells, left_cells = (
            jnp.concatenate([a, jnp.where(sub8 == 7, b, c)], 0)
            for a, b, c in zip(sides, over, under)
        )
        for lg in range(8):
            near_r = pltpu.roll(right_cells, 128 - 16 * lg, 1) if lg else right_cells
            near_l = pltpu.roll(left_cells, (144 - 16 * lg) % 128, 1) if lg != 1 else left_cells
            side_raw[9 * lg + q] = jnp.where(lane24 < 16, near_r, near_l)
        return carry

    lax.fori_loop(0, 9, gather_edges, 0)

    pltpu.make_async_copy(rep_in.at[pl.ds(0, DEV - 1)], rep_in.at[pl.ds(0, DEV - 1)], rep_r).wait()
    last = rep_in[:, 3, :]
    for k in range(CAP):
        main = rep_in[:, k // 2, :]
        if k % 2:
            main = pltpu.roll(main, 64, 1)
        shift = (64 - 16 * k) % 128
        end = pltpu.roll(last, shift, 1) if shift else last
        cols = jnp.where(lane128 < 64, main, jnp.where(lane128 < VALS, end, 0.0))
        hi, lo = split2(cols.T[:VALS])
        dsplit[pl.ds(0, VALS), pl.ds(k * DEV, DEV)] = hi
        dsplit[pl.ds(VALS, VALS), pl.ds(k * DEV, DEV)] = lo

    def assemble(i, carry):
        cols = pl.ds(pl.multiple_of(i * 2 * CY, 2 * CY), 2 * CY)
        two = jnp.dot(dsplit[...], onehot[:, cols], preferred_element_type=F32)
        full = kv_own[:, cols] + two[:VALS] + two[VALS:]
        kv[:, 2 * i, :] = full[:, :CY]
        kv[:, 2 * i + 1, :] = full[:, CY:]
        return carry

    for i in range(CX // 2):
        assemble(i, 0)

    for g in range(3):
        acc = jnp.zeros((CX, CY), F32)
        for m in range(32 if g < 2 else VALS - 64):
            moved = pltpu.roll(kv[32 * g + m], 4 * m + 2, 1) if 4 * m + 2 < 128 else kv[32 * g + m]
            acc = jnp.where(lane16 // 4 == m, moved, acc)
        edge_kv[g] = acc
    kvedges = to_sides((edge_kv, edge_kv), edge_kv_in, kvedge_s, kvedge_r)
    kvrows = [
        pltpu.make_async_remote_copy(
            kv.at[:, pl.ds(14, 2), :], kv_halo.at[:, pl.ds(6, 2), :],
            kvrow_s.at[0], kvrow_r.at[0], device_id=(down, fy), device_id_type=MESH,
        ),
        pltpu.make_async_remote_copy(
            kv.at[:, pl.ds(0, 2), :], kv_halo.at[:, pl.ds(0, 2), :],
            kvrow_s.at[1], kvrow_r.at[1], device_id=(up, fy), device_id_type=MESH,
        ),
    ]
    for copy in kvrows:
        copy.start()

    def factors(before, after, share):
        rest = 1.0 + before * share
        inverse = 1.0 / (rest + after)
        return after * inverse, inverse, rest * inverse

    def solve(*systems):
        def inwards(step, carry):
            done = []
            for (coupling, ratios, right_sides, count, put, _), state in zip(systems, carry):
                for (before, share, partial), level, nearer in zip(
                    state, (step, LEV - 1 - step), (step, LEV - 2 - step)
                ):
                    after = coupling[nearer]
                    ratio, inverse, share = factors(before, after, share)
                    ratios[level] = ratio
                    new = []
                    for j in range(count):
                        g = (right_sides(level, j) + before * partial[j]) * inverse
                        put(level, j, g)
                        new.append(g)
                    done.append((after, share, tuple(new)))
            return tuple(zip(done[0::2], done[1::2]))

        start = []
        for coupling, _, _, count, _, _ in systems:
            last = coupling[LEV - 1]
            zero = jnp.zeros_like(last)
            zeros = (zero,) * count
            start.append(((zero, zero + 1.0, zeros), (last, zero + 1.0, zeros)))
        met = lax.fori_loop(0, LEV // 2, inwards, tuple(start))
        high, low = LEV // 2 - 1, LEV // 2
        ends = []
        for (_, ratios, _, count, put, _), ((_, _, top), (_, _, bottom)) in zip(systems, met):
            e, f = ratios[high], ratios[low]
            scale = 1.0 / (1.0 - e * f)
            above, below = [], []
            for j in range(count):
                x = (top[j] + e * bottom[j]) * scale
                y = bottom[j] + f * x
                put(high, j, x)
                put(low, j, y)
                above.append(x)
                below.append(y)
            ends.append((tuple(above), tuple(below)))

        def outwards(step, carry):
            done = []
            for (_, ratios, _, count, put, get), state in zip(systems, carry):
                for last, level in zip(state, (high - 1 - step, low + 1 + step)):
                    ratio = ratios[level]
                    new = []
                    for j in range(count):
                        x = get(level, j) + ratio * last[j]
                        put(level, j, x)
                        new.append(x)
                    done.append(tuple(new))
            return tuple(zip(done[0::2], done[1::2]))

        lax.fori_loop(0, LEV // 2 - 1, outwards, tuple(ends))

    for t in range(TR):
        tv[t, LEV - 1] = tv[t, LEV - 1] + kv[LEV + t]

    def put_own(level, t, x):
        ue[level, pl.ds(STRIDE * t + 8, CX), :] = x

    solve(
        (kv, ratio_own, lambda level, t: tv[t, level], TR, put_own,
         lambda level, t: ue[level, pl.ds(STRIDE * t + 8, CX), :])
    )

    group = 36

    def mix(b, carry):
        for n in range(group):
            for t in range(TR):
                at = pl.ds((n * TR + t) * CX, CX)
                hi, lo = split2(ue[b * group + n, pl.ds(STRIDE * t + 8, CX), :])
                parts[at, pl.ds(0, CY)] = hi
                parts[at, pl.ds(CY, CY)] = lo
        mixed = jnp.dot(parts[...], weights[...], preferred_element_type=F32)
        for n in range(group):
            for t in range(TR):
                own = pl.ds(STRIDE * t + 8, CX)
                at = (n * TR + t) * CX
                both = mixed[at : at + CX]
                ub[b * group + n, own, :] = both[:, CY:]
        for n in range(group):
            for t in range(TR):
                level, row = b * group + n, STRIDE * t + 8
                at = (n * TR + t) * CX
                near = ub[level, pl.ds(row - 1, CX), :] + ub[level, pl.ds(row + 1, CX), :]
                far = ue[level, pl.ds(row - 2, CX), :] + ue[level, pl.ds(row + 2, CX), :]
                ua[level, pl.ds(t * CX, CX), :] = ue[level, pl.ds(row, CX), :] - 0.025 * (
                    (far + near) + mixed[at : at + CX, :CY]
                )
        return carry

    lax.fori_loop(0, LEV // group, mix, 0)

    for copy in kvrows + kvedges:
        copy.wait_recv()
    for copy in rows:
        copy.wait_recv()
    for g in range(3):
        edge_kv_all[g, pl.ds(0, CX), :] = jnp.where(lane16 % 4 < 2, edge_kv_in[0, g], edge_kv_in[1, g])
        over = jnp.where(lane8 % 4 < 2, edge_kv_in[2, g, pl.ds(8, 8)], edge_kv_in[3, g, pl.ds(8, 8)])
        under = jnp.where(lane8 % 4 < 2, edge_kv_in[4, g, pl.ds(0, 8)], edge_kv_in[5, g, pl.ds(0, 8)])
        edge_kv_all[g, pl.ds(CX, 8), :] = jnp.where(sub8 == 7, over, under)
    quad = jnp.where(lane24 % 32 < 16, 2, 0) + lane24 % 2

    for level in range(LEV):
        side_kv[level] = jnp.take_along_axis(
            edge_kv_all[level // 32], 4 * (level % 32) + quad, axis=1
        )

    side_flux = jnp.take_along_axis(
        edge_kv_all[2], 32 + 4 * ((lane24 % 16) // 2) + quad, axis=1
    )

    for j in range(TR + 1):
        tile = pl.ds(8 * j, 8)
        halo[LEV - 1, tile, :] = halo[LEV - 1, tile, :] + jnp.where(
            sub8 < 4, kv_halo[LEV + max(j - 1, 0)], kv_halo[LEV + min(j, TR - 1)]
        )
    side_raw[LEV - 1] = side_raw[LEV - 1] + side_flux

    def put_rows(level, j, x):
        ue[level, pl.ds(STRIDE * j, 8), :] = x

    def put_side(level, j, x):
        us[level, pl.ds(8, 24), :] = x
        us[level, pl.ds(0, 8), :] = x[CX:]

    solve(
        (kv_halo, ratio_halo, lambda level, j: halo[level, pl.ds(8 * j, 8), :], TR + 1, put_rows,
         lambda level, j: ue[level, pl.ds(STRIDE * j, 8), :]),
        (side_kv, ratio_side, lambda level, j: side_raw[level], 1, put_side,
         lambda level, j: us[level, pl.ds(8, 24), :]),
    )

    for level in range(LEV):
        rim = jnp.concatenate(
            [ue[level, pl.ds(7, TR, stride=STRIDE), :], ue[level, pl.ds(STRIDE, TR, stride=STRIDE), :]], 0
        )
        hi, lo = split2(rim)
        parts[pl.ds(level * 2 * TR, 2 * TR), pl.ds(0, CY)] = hi
        parts[pl.ds(level * 2 * TR, 2 * TR), pl.ds(CY, CY)] = lo
    fixed = jnp.dot(parts[pl.ds(0, LEV * 2 * TR), :], weights[:, pl.ds(CY, CY)], preferred_element_type=F32)
    for level in range(LEV):
        at = level * 2 * TR
        def beside(row):
            return ue[level, pl.ds(row, TR, stride=STRIDE), :]

        for row, add in (
            (0, fixed[at : at + TR] + beside(6)),
            (1, beside(7)),
            (CX - 2, beside(STRIDE)),
            (CX - 1, fixed[at + TR : at + 2 * TR] + beside(STRIDE + 1)),
        ):
            place = pl.ds(row, TR, stride=CX)
            ua[level, place, :] = ua[level, place, :] - 0.025 * add

    for copy in rows + edges + kvrows + kvedges:
        copy.wait_send()
    pltpu.make_async_copy(req.at[pl.ds(0, DEV - 1)], req.at[pl.ds(0, DEV - 1)], req_s).wait()
    pltpu.make_async_copy(rep.at[pl.ds(0, DEV - 1)], rep.at[pl.ds(0, DEV - 1)], rep_s).wait()


def smooth_kernel(us, ua, out, held, side_weights, side_out, sem):
    row, col = iota((CY, CY), 0), iota((CY, CY), 1)
    goal = (row % 32) // 16 * 2 + row % 2
    for t in range(TR):
        hit = (row < 64) & ((row % 16) // 2 == t) & (col == (goal + CY - 2) % CY)
        side_weights[:, pl.ds(t * CY, CY)] = jnp.where(hit, 1.0, 0.0).astype(BF16)

    def sides(start, levels):
        height = levels * CX

        def cells(first):
            return us[pl.ds(start, levels), pl.ds(first, CX), :].reshape(height, CY)

        lane = iota((height, CY), 1)
        u = cells(8)
        q = 2.0 * (cells(7) + cells(9)) - 8.0 * u
        across = jnp.where(
            lane < 16,
            jnp.where(lane % 2 == 1, pltpu.roll(q, 1, 1), 0.0),
            jnp.where(lane % 2 == 0, pltpu.roll(q, CY - 1, 1), 0.0),
        )
        side = u + across
        rest = side - side.astype(BF16).astype(F32)
        both = jnp.where(lane < 32, side, jnp.where(lane < 64, pltpu.roll(rest, 32, 1), 0.0))
        side_out[pl.ds(start * CX, height), :] = jnp.dot(
            both.astype(BF16), side_weights[...], preferred_element_type=F32
        )

    copies = []
    first = 0
    for block, count in enumerate((12, 12, 12, 12, 12, 6, 4, 2)):
        if block == 0:
            sides(0, count)
        if block == 1:
            sides(count, LEV - count)
        for level in range(first, first + count):
            for t in range(TR):
                edge = side_out[pl.ds(level * CX, CX), pl.ds(t * CY, CY)]
                held[t, level] = ua[level, pl.ds(t * CX, CX), :] - 0.025 * edge
        levels = pl.ds(first, count)
        first += count
        copy = pltpu.make_async_copy(held.at[:, levels], out.at[:, levels], sem.at[block])
        copy.start()
        copies.append(copy)
    for copy in copies:
        copy.wait()


def local(tracers, group_dest, group_slot, diffusivity, surface_flux):
    any_spec = pl.BlockSpec(memory_space=pltpu.HBM)
    dma = pltpu.SemaphoreType.DMA
    us, ua = pl.pallas_call(
        exchange_kernel,
        out_shape=(
            pltpu.VMEM((LEV, 32, CY), F32),
            pltpu.VMEM((LEV, TR * CX, CY), F32),
        ),
        in_specs=[any_spec] * 5,
        out_specs=(pl.BlockSpec(memory_space=pltpu.VMEM),) * 2,
        scratch_shapes=[
            pltpu.VMEM((LEV, UROWS, CY), F32),
            pltpu.VMEM((LEV, UROWS, CY), F32),
            pltpu.VMEM((TR, LEV, CX, CY), F32),
            pltpu.VMEM((CX, CY), jnp.int32),
            pltpu.VMEM((CX, CY), jnp.int32),
            pltpu.VMEM((VALS, SLOTS), F32),
            pltpu.VMEM((SLOTS, 256), BF16),
            pltpu.VMEM((CAP * DEV, SLOTS), BF16),
            pltpu.VMEM((SLOTS, 256), BF16),
            pltpu.VMEM((CX, CY), F32),
            pltpu.VMEM((DEV, SLOTS), BF16),
            pltpu.VMEM((16, SLOTS), BF16),
            pltpu.VMEM((CAP * DEV, SLOTS), BF16),
            pltpu.VMEM((DEV, 2 * CAP * CY), BF16),
            pltpu.VMEM((DEV, 1, CY), F32),
            pltpu.VMEM((DEV, 1, CY), F32),
            pltpu.VMEM((DEV, 4, CY), F32),
            pltpu.VMEM((DEV, 4, CY), F32),
            pltpu.VMEM((2 * VALS, CAP * DEV), BF16),
            pltpu.VMEM((VALS, SLOTS), F32),
            pltpu.VMEM((VALS, CX, CY), F32),
            pltpu.VMEM((3, CX, CY), F32),
            pltpu.VMEM((6, 3, CX, CY), F32),
            pltpu.VMEM((VALS, 8, CY), F32),
            pltpu.VMEM((LEV, 8 * (TR + 1), CY), F32),
            pltpu.VMEM((2, 9, CX, CY), F32),
            pltpu.VMEM((6, 9, CX, CY), F32),
            pltpu.VMEM((LEV, 24, CY), F32),
            pltpu.VMEM((LEV, 24, CY), F32),
            pltpu.VMEM((3, 24, CY), F32),
            pltpu.VMEM((LEV, CX, CY), F32),
            pltpu.VMEM((LEV, 8, CY), F32),
            pltpu.VMEM((LEV, 24, CY), F32),
            pltpu.VMEM((36 * TR * CX, 2 * CY), BF16),
            pltpu.VMEM((2 * CY, 2 * CY), BF16),
            dma((4,)), dma, dma, dma, dma, dma,
            dma((2 * TR,)), dma((2 * TR,)), dma((6,)), dma((6,)),
            dma((2,)), dma((2,)), dma((6,)), dma((6,)),
        ],
        compiler_params=pltpu.CompilerParams(
            collective_id=0, has_side_effects=True, vmem_limit_bytes=48 << 20
        ),
        name="exchange",
    )(
        *(
            pltpu.with_memory_space_constraint(x, pltpu.HBM)
            for x in (tracers, group_dest, group_slot, diffusivity, surface_flux)
        )
    )
    whole = pl.BlockSpec(memory_space=pltpu.VMEM)
    return pl.pallas_call(
        smooth_kernel,
        out_shape=jax.ShapeDtypeStruct(tracers.shape, F32),
        in_specs=[whole] * 2,
        out_specs=pl.BlockSpec(memory_space=pl.ANY),
        scratch_shapes=[
            pltpu.VMEM((TR, LEV, CX, CY), F32),
            pltpu.VMEM((CY, TR * CY), BF16),
            pltpu.VMEM((LEV * CX, TR * CY), F32),
            dma((8,)),
        ],
        compiler_params=pltpu.CompilerParams(vmem_limit_bytes=16 << 20),
        name="smooth",
    )(us, ua)


def solution(mesh):
    placed = (
        P(None, None, "fx", "fy"),
        P("fx", "fy"),
        P("fx", "fy"),
        P(None, ("fx", "fy")),
        P(None, ("fx", "fy")),
    )
    return jax.shard_map(
        local, mesh=mesh, in_specs=placed, out_specs=P(None, None, "fx", "fy"), check_vma=False
    )
```

```python
import jax
import jax.numpy as jnp
from jax import lax
from jax.experimental import pallas as pl
from jax.experimental.pallas import tpu as pltpu
from jax.sharding import PartitionSpec as P

MESH = pl.DeviceIdType.MESH
F32 = jnp.float32
BF16 = jnp.bfloat16
CAP = 6
N_FX, N_FY, DEV = 8, 16, 128
TR, LEV, CX, CY = 8, 72, 16, 128
SLOTS = 2048
VALS = LEV + TR
STRIDE = 24
UROWS = TR * STRIDE + 8


def iota(shape, dim):
    return lax.broadcasted_iota(jnp.int32, shape, dim)


def split2(x):
    hi = x.astype(BF16)
    lo = (x - hi.astype(F32)).astype(BF16)
    return hi, lo


def split3(x):
    hi = x.astype(BF16)
    rest = x - hi.astype(F32)
    mid = rest.astype(BF16)
    lo = (rest - mid.astype(F32)).astype(BF16)
    return hi, mid, lo


HOPS = (0, 1, 2, 1)
STEPS = sorted(
    (
        (dz, dx, dy, dc)
        for dz in range(4) for dx in range(4) for dy in range(4) for dc in range(2)
        if dz or dx or dy or dc
    ),
    key=lambda d: -(HOPS[d[0]] + HOPS[d[1]] + HOPS[d[2]]),
)


def all_peers(fx, fy):
    z, core, x, y = fx // 2, fx % 2, fy // 4, fy % 4
    zs, cores = [(z + d) % 4 * 2 for d in range(4)], [core, 1 - core]
    xs, ys = [(x + d) % 4 * 4 for d in range(4)], [(y + d) % 4 for d in range(4)]
    on_fx = {(dz, dc): zs[dz] + cores[dc] for dz in range(4) for dc in range(2)}
    on_fy = {(dx, dy): xs[dx] + ys[dy] for dx in range(4) for dy in range(4)}
    return [(on_fx[dz, dc], on_fy[dx, dy]) for dz, dx, dy, dc in STEPS]


def exchange_kernel(
    tracers, dest, slot, diff, flux,
    us, ua,
    ue, ub, tv, dest_v, slot_v, table, table_t, onehot, onehot_own, rank_v,
    matches, picks, chosen, widen, req, req_in, rep, rep_in, dsplit, kv_own, kv, edge_kv, edge_kv_in, kv_halo,
    halo, edge, edge_in, side_raw, side_kv, edge_kv_all, ratio_own, ratio_halo, ratio_side, parts, weights,
    load_sem, tv_sem, req_s, req_r, rep_s, rep_r, row_s, row_r, edge_s, edge_r,
    kvrow_s, kvrow_r, kvedge_s, kvedge_r,
):
    fx, fy = lax.axis_index("fx"), lax.axis_index("fy")
    me = fx * N_FY + fy
    up, down = (fx + N_FX - 1) % N_FX, (fx + 1) % N_FX
    left, right = (fy + N_FY - 1) % N_FY, (fy + 1) % N_FY

    loads = [
        pltpu.make_async_copy(dest, dest_v, load_sem.at[0]),
        pltpu.make_async_copy(slot, slot_v, load_sem.at[1]),
        pltpu.make_async_copy(diff, table.at[pl.ds(0, LEV)], load_sem.at[2]),
        pltpu.make_async_copy(flux, table.at[pl.ds(LEV, TR)], load_sem.at[3]),
    ]
    for load in loads:
        load.start()
    tv_load = pltpu.make_async_copy(tracers, tv, tv_sem)
    tv_load.start()

    barrier = pltpu.get_barrier_semaphore()
    peers = all_peers(fx, fy)

    def each_peer(action):
        for px, py in peers:
            action(px, py)

    def hello(px, py):
        pl.semaphore_signal(barrier, inc=1, device_id=(px, py), device_id_type=MESH)

    each_peer(hello)

    loads[0].wait()
    loads[1].wait()
    lane128 = iota((DEV, CY), 1)
    sub128 = iota((DEV, CY), 0)
    prefix = jnp.concatenate(
        [jnp.where(sub128 < lane128, 1.0, 0.0), jnp.ones((DEV, CY), F32)], 1
    ).astype(BF16)

    kk = iota((16, CY), 0)
    seen = jnp.zeros((DEV, CY), F32)
    for i in range(CX):
        d = dest_v[pl.ds(i, 1), :]
        d = jnp.where(d == me, -1, d)
        slots = slot_v[pl.ds(i, 1), :]
        match = jnp.where(d == sub128, 1.0, 0.0)
        mb = match.astype(BF16)
        matches[:, pl.ds(i * CY, CY)] = mb
        counts = jnp.dot(mb, prefix, preferred_element_type=F32)
        rank = jnp.sum(match * (counts[:, :CY] + seen), axis=0, keepdims=True)
        seen = seen + counts[:, CY:]
        rank_v[pl.ds(i, 1), :] = rank
        value = jnp.where(kk < 8, (slots >> 7) + 1, slots & 127).astype(F32)
        picks[:, pl.ds(i * CY, CY)] = jnp.where((kk & 7).astype(F32) == rank, value, 0.0).astype(BF16)
    asked = lax.dot_general(
        matches[...], picks[...], (((1,), (1,)), ((), ())), preferred_element_type=F32
    )
    req[:, 0, :] = jnp.concatenate([asked, jnp.zeros((DEV, CY - 16), F32)], 1)

    loads[2].wait()
    loads[3].wait()

    def flip(b, carry):
        cols = pl.ds(pl.multiple_of(b * 128, 128), 128)
        part = jnp.concatenate([table[:, cols], jnp.zeros((128 - VALS, 128), F32)], 0)
        hi, lo = split2(part.T)
        table_t[cols, pl.ds(0, 128)] = hi
        table_t[cols, pl.ds(128, 128)] = lo
        return carry

    lax.fori_loop(0, SLOTS // 128, flip, 0)

    for m in range(2 * CAP):
        lane_of = m if m < CAP else 8 + m - CAP
        widen[:, pl.ds(m * CY, CY)] = jnp.where(sub128 == lane_of, 1.0, 0.0).astype(BF16)

    def spread(i, carry):
        cols = pl.ds(pl.multiple_of(i * CY, CY), CY)
        d = dest_v[pl.ds(i, 1), :]
        d = jnp.where(d == me, -1, d)
        rank = rank_v[pl.ds(i, 1), :]
        hit = d == sub128
        for k in range(CAP):
            onehot[pl.ds(k * DEV, DEV), cols] = jnp.where(
                hit & (rank == float(k)), 1.0, 0.0
            ).astype(BF16)
        return carry

    lax.fori_loop(0, CX, spread, 0)
    pl.semaphore_wait(barrier, DEV - 1)

    def ask(px, py):
        pltpu.make_async_remote_copy(
            req.at[px * N_FY + py], req_in.at[me], req_s, req_r,
            device_id=(px, py), device_id_type=MESH,
        ).start()

    each_peer(ask)
    req_in[me] = jnp.zeros((1, CY), F32)

    rows = []
    for t in range(TR):
        rows.append(
            pltpu.make_async_remote_copy(
                tracers.at[t, :, pl.ds(14, 2), :],
                halo.at[:, pl.ds(8 * t + 6, 2), :],
                row_s.at[t], row_r.at[t], device_id=(down, fy), device_id_type=MESH,
            )
        )
        rows.append(
            pltpu.make_async_remote_copy(
                tracers.at[t, :, pl.ds(0, 2), :],
                halo.at[:, pl.ds(8 * t + 8, 2), :],
                row_s.at[TR + t], row_r.at[TR + t], device_id=(up, fy), device_id_type=MESH,
            )
        )
    for copy in rows:
        copy.start()

    tv_load.wait()
    lane16 = iota((CX, CY), 1)

    def pack(q, carry):
        first = last = jnp.zeros((CX, CY), F32)
        for lg in range(8):
            for t in range(TR):
                cells = tv[t, q + 9 * lg]
                at = 16 * lg + 2 * t
                here = (lane16 == at) | (lane16 == at + 1)
                first = jnp.where(here, pltpu.roll(cells, at, 1) if at else cells, first)
                moved = pltpu.roll(cells, (at + 2) % 128, 1) if (at + 2) % 128 else cells
                last = jnp.where(here, moved, last)
        edge[0, q] = last
        edge[1, q] = first
        return carry

    lax.fori_loop(0, 9, pack, 0)

    def to_sides(sources, target, sends, receives):
        places = [
            (fx, right, 0, 0, CX), (fx, left, 1, 0, CX),
            (down, right, 2, CX - 1, 1), (down, left, 3, CX - 1, 1),
            (up, right, 4, 0, 1), (up, left, 5, 0, 1),
        ]
        copies = [
            pltpu.make_async_remote_copy(
                sources[n % 2].at[:, pl.ds(first, count), :],
                target.at[n, :, pl.ds(first, count), :],
                sends.at[n], receives.at[n], device_id=(px, py), device_id_type=MESH,
            )
            for px, py, n, first, count in places
        ]
        for copy in copies[2:] + copies[:2]:
            copy.start()
        return copies

    edges = to_sides((edge.at[0], edge.at[1]), edge_in, edge_s, edge_r)

    gap = jnp.abs(sub128 - lane128)
    first = jnp.where(gap == 0, 20.0, jnp.where(gap == 1, -8.0, jnp.where(gap == 2, 1.0, 0.0)))
    second = jnp.where(gap == 0, -8.0, jnp.where(gap == 1, 2.0, 0.0))
    for n in range(2):
        weights[pl.ds(n * CY, CY), pl.ds(0, CY)] = first.astype(BF16)
        weights[pl.ds(n * CY, CY), pl.ds(CY, CY)] = second.astype(BF16)

    def clear(level, carry):
        for j in range(TR + 1):
            ue[level, pl.ds(STRIDE * j, 8), :] = jnp.zeros((8, CY), F32)
            ub[level, pl.ds(STRIDE * j, 8), :] = jnp.zeros((8, CY), F32)
        return carry

    lax.fori_loop(0, LEV, clear, 0)

    pltpu.make_async_copy(req_in.at[pl.ds(0, DEV - 1)], req_in.at[pl.ds(0, DEV - 1)], req_r).wait()
    wanted = req_in[:, 0, :]
    zero_b = jnp.zeros((DEV, CY), BF16)
    zero_f = jnp.zeros((DEV, CY), F32)
    lane_f = lane128.astype(F32)
    apart = jnp.dot(wanted.astype(BF16), widen[...], preferred_element_type=F32)
    for k in range(CAP):
        high = apart[:, k * CY : (k + 1) * CY].astype(BF16)
        low = jnp.where(apart[:, (CAP + k) * CY : (CAP + k + 1) * CY] == lane_f, 1.0, 0.0).astype(BF16)
        for b in range(SLOTS // 128):
            chosen[pl.ds(k * DEV, DEV), pl.ds(b * 128, 128)] = jnp.where(high == float(b + 1), low, zero_b)
    both = jnp.dot(chosen[...], table_t[...], preferred_element_type=F32)
    both = both[:, :128] + both[:, 128:]
    got = [both[k * DEV : (k + 1) * DEV] for k in range(CAP)]
    for j in range(3):
        rep[:, j, :] = jnp.where(lane128 < 64, got[2 * j], pltpu.roll(got[2 * j + 1], 64, 1))
    tail = jnp.zeros((DEV, CY), F32)
    for k in range(CAP):
        shift = (16 * k - 64) % 128
        moved = pltpu.roll(got[k], shift, 1) if shift else got[k]
        tail = jnp.where(lane128 // 16 == k, moved, tail)
    rep[:, 3, :] = tail

    def answer(px, py):
        pltpu.make_async_remote_copy(
            rep.at[px * N_FY + py], rep_in.at[me], rep_s, rep_r,
            device_id=(px, py), device_id_type=MESH,
        ).start()

    each_peer(answer)
    rep_in[me] = jnp.zeros((4, CY), F32)

    tab3 = jnp.concatenate(split3(table[...]), 0)

    def keep(i, carry):
        for half in range(2):
            d = dest_v[pl.ds(2 * i + half, 1), :]
            s = jnp.where(d == me, slot_v[pl.ds(2 * i + half, 1), :], -1)
            high = ((s >> 7).astype(F32) + zero_f).astype(BF16)
            low = jnp.where((s & 127) == sub128, 1.0, 0.0).astype(BF16)
            for b in range(SLOTS // 128):
                onehot_own[pl.ds(b * 128, 128), pl.ds(half * CY, CY)] = jnp.where(
                    high == float(b), low, zero_b
                )
        three = jnp.dot(tab3, onehot_own[...], preferred_element_type=F32)
        kv_own[:, pl.ds(pl.multiple_of(i * 2 * CY, 2 * CY), 2 * CY)] = (
            three[:VALS] + three[VALS : 2 * VALS] + three[2 * VALS :]
        )
        return carry

    lax.fori_loop(0, CX // 2, keep, 0)

    for copy in edges:
        copy.wait_recv()
    lane8 = iota((8, CY), 1)
    sub8 = iota((8, CY), 0)
    lane24 = iota((24, CY), 1)

    def gather_edges(q, carry):
        def merged(n, rows):
            return edge_in[n + 1, q, rows], edge_in[n, q, rows]

        sides = merged(0, pl.ds(0, CX))
        over = merged(2, pl.ds(8, 8))
        under = merged(4, pl.ds(0, 8))
        right_cells, left_cells = (
            jnp.concatenate([a, jnp.where(sub8 == 7, b, c)], 0)
            for a, b, c in zip(sides, over, under)
        )
        for lg in range(8):
            near_r = pltpu.roll(right_cells, 128 - 16 * lg, 1) if lg else right_cells
            near_l = pltpu.roll(left_cells, (144 - 16 * lg) % 128, 1) if lg != 1 else left_cells
            side_raw[9 * lg + q] = jnp.where(lane24 < 16, near_r, near_l)
        return carry

    lax.fori_loop(0, 9, gather_edges, 0)

    pltpu.make_async_copy(rep_in.at[pl.ds(0, DEV - 1)], rep_in.at[pl.ds(0, DEV - 1)], rep_r).wait()
    last = rep_in[:, 3, :]
    for k in range(CAP):
        main = rep_in[:, k // 2, :]
        if k % 2:
            main = pltpu.roll(main, 64, 1)
        shift = (64 - 16 * k) % 128
        end = pltpu.roll(last, shift, 1) if shift else last
        cols = jnp.where(lane128 < 64, main, jnp.where(lane128 < VALS, end, 0.0))
        hi, lo = split2(cols.T[:VALS])
        dsplit[pl.ds(0, VALS), pl.ds(k * DEV, DEV)] = hi
        dsplit[pl.ds(VALS, VALS), pl.ds(k * DEV, DEV)] = lo

    def assemble(i, carry):
        cols = pl.ds(pl.multiple_of(i * 2 * CY, 2 * CY), 2 * CY)
        two = jnp.dot(dsplit[...], onehot[:, cols], preferred_element_type=F32)
        full = kv_own[:, cols] + two[:VALS] + two[VALS:]
        kv[:, 2 * i, :] = full[:, :CY]
        kv[:, 2 * i + 1, :] = full[:, CY:]
        return carry

    for i in range(CX // 2):
        assemble(i, 0)

    for g in range(3):
        acc = jnp.zeros((CX, CY), F32)
        for m in range(32 if g < 2 else VALS - 64):
            moved = pltpu.roll(kv[32 * g + m], 4 * m + 2, 1) if 4 * m + 2 < 128 else kv[32 * g + m]
            acc = jnp.where(lane16 // 4 == m, moved, acc)
        edge_kv[g] = acc
    kvedges = to_sides((edge_kv, edge_kv), edge_kv_in, kvedge_s, kvedge_r)
    kvrows = [
        pltpu.make_async_remote_copy(
            kv.at[:, pl.ds(14, 2), :], kv_halo.at[:, pl.ds(6, 2), :],
            kvrow_s.at[0], kvrow_r.at[0], device_id=(down, fy), device_id_type=MESH,
        ),
        pltpu.make_async_remote_copy(
            kv.at[:, pl.ds(0, 2), :], kv_halo.at[:, pl.ds(0, 2), :],
            kvrow_s.at[1], kvrow_r.at[1], device_id=(up, fy), device_id_type=MESH,
        ),
    ]
    for copy in kvrows:
        copy.start()

    def factors(before, after, share):
        rest = 1.0 + before * share
        inverse = 1.0 / (rest + after)
        return after * inverse, inverse, rest * inverse

    def solve(*systems):
        def inwards(step, carry):
            done = []
            for (coupling, ratios, right_sides, count, put, _), state in zip(systems, carry):
                for (before, share, partial), level, nearer in zip(
                    state, (step, LEV - 1 - step), (step, LEV - 2 - step)
                ):
                    after = coupling[nearer]
                    ratio, inverse, share = factors(before, after, share)
                    ratios[level] = ratio
                    new = []
                    for j in range(count):
                        g = (right_sides(level, j) + before * partial[j]) * inverse
                        put(level, j, g)
                        new.append(g)
                    done.append((after, share, tuple(new)))
            return tuple(zip(done[0::2], done[1::2]))

        start = []
        for coupling, _, _, count, _, _ in systems:
            last = coupling[LEV - 1]
            zero = jnp.zeros_like(last)
            zeros = (zero,) * count
            start.append(((zero, zero + 1.0, zeros), (last, zero + 1.0, zeros)))
        met = lax.fori_loop(0, LEV // 2, inwards, tuple(start))
        high, low = LEV // 2 - 1, LEV // 2
        ends = []
        for (_, ratios, _, count, put, _), ((_, _, top), (_, _, bottom)) in zip(systems, met):
            e, f = ratios[high], ratios[low]
            scale = 1.0 / (1.0 - e * f)
            above, below = [], []
            for j in range(count):
                x = (top[j] + e * bottom[j]) * scale
                y = bottom[j] + f * x
                put(high, j, x)
                put(low, j, y)
                above.append(x)
                below.append(y)
            ends.append((tuple(above), tuple(below)))

        def outwards(step, carry):
            done = []
            for (_, ratios, _, count, put, get), state in zip(systems, carry):
                for last, level in zip(state, (high - 1 - step, low + 1 + step)):
                    ratio = ratios[level]
                    new = []
                    for j in range(count):
                        x = get(level, j) + ratio * last[j]
                        put(level, j, x)
                        new.append(x)
                    done.append(tuple(new))
            return tuple(zip(done[0::2], done[1::2]))

        lax.fori_loop(0, LEV // 2 - 1, outwards, tuple(ends))

    for t in range(TR):
        tv[t, LEV - 1] = tv[t, LEV - 1] + kv[LEV + t]

    def put_own(level, t, x):
        ue[level, pl.ds(STRIDE * t + 8, CX), :] = x

    solve(
        (kv, ratio_own, lambda level, t: tv[t, level], TR, put_own,
         lambda level, t: ue[level, pl.ds(STRIDE * t + 8, CX), :])
    )

    group = 36

    def mix(b, carry):
        for n in range(group):
            for t in range(TR):
                at = pl.ds((n * TR + t) * CX, CX)
                hi, lo = split2(ue[b * group + n, pl.ds(STRIDE * t + 8, CX), :])
                parts[at, pl.ds(0, CY)] = hi
                parts[at, pl.ds(CY, CY)] = lo
        mixed = jnp.dot(parts[...], weights[...], preferred_element_type=F32)
        for n in range(group):
            for t in range(TR):
                own = pl.ds(STRIDE * t + 8, CX)
                at = (n * TR + t) * CX
                both = mixed[at : at + CX]
                ub[b * group + n, own, :] = both[:, CY:]
        for n in range(group):
            for t in range(TR):
                level, row = b * group + n, STRIDE * t + 8
                at = (n * TR + t) * CX
                near = ub[level, pl.ds(row - 1, CX), :] + ub[level, pl.ds(row + 1, CX), :]
                far = ue[level, pl.ds(row - 2, CX), :] + ue[level, pl.ds(row + 2, CX), :]
                ua[level, pl.ds(t * CX, CX), :] = ue[level, pl.ds(row, CX), :] - 0.025 * (
                    (far + near) + mixed[at : at + CX, :CY]
                )
        return carry

    lax.fori_loop(0, LEV // group, mix, 0)

    quad = jnp.where(lane24 % 32 < 16, 2, 0) + lane24 % 2

    def spread_kv(rows, index):
        for level in range(LEV):
            side_kv[level, rows, :] = jnp.take_along_axis(
                edge_kv_all[level // 32, rows, :], 4 * (level % 32) + index, axis=1
            )

    for copy in kvedges[:2]:
        copy.wait_recv()
    for g in range(3):
        edge_kv_all[g, pl.ds(0, CX), :] = jnp.where(lane16 % 4 < 2, edge_kv_in[0, g], edge_kv_in[1, g])
    spread_kv(pl.ds(0, CX), quad[:CX])
    for copy in kvrows + kvedges[2:] + rows:
        copy.wait_recv()
    for g in range(3):
        over = jnp.where(lane8 % 4 < 2, edge_kv_in[2, g, pl.ds(8, 8)], edge_kv_in[3, g, pl.ds(8, 8)])
        under = jnp.where(lane8 % 4 < 2, edge_kv_in[4, g, pl.ds(0, 8)], edge_kv_in[5, g, pl.ds(0, 8)])
        edge_kv_all[g, pl.ds(CX, 8), :] = jnp.where(sub8 == 7, over, under)
    spread_kv(pl.ds(CX, 8), quad[CX:])

    side_flux = jnp.take_along_axis(
        edge_kv_all[2], 32 + 4 * ((lane24 % 16) // 2) + quad, axis=1
    )

    for j in range(TR + 1):
        tile = pl.ds(8 * j, 8)
        halo[LEV - 1, tile, :] = halo[LEV - 1, tile, :] + jnp.where(
            sub8 < 4, kv_halo[LEV + max(j - 1, 0)], kv_halo[LEV + min(j, TR - 1)]
        )
    side_raw[LEV - 1] = side_raw[LEV - 1] + side_flux

    def put_rows(level, j, x):
        ue[level, pl.ds(STRIDE * j, 8), :] = x

    def put_side(level, j, x):
        us[level, pl.ds(8, 24), :] = x
        us[level, pl.ds(0, 8), :] = x[CX:]

    solve(
        (kv_halo, ratio_halo, lambda level, j: halo[level, pl.ds(8 * j, 8), :], TR + 1, put_rows,
         lambda level, j: ue[level, pl.ds(STRIDE * j, 8), :]),
        (side_kv, ratio_side, lambda level, j: side_raw[level], 1, put_side,
         lambda level, j: us[level, pl.ds(8, 24), :]),
    )

    for level in range(LEV):
        rim = jnp.concatenate(
            [ue[level, pl.ds(7, TR, stride=STRIDE), :], ue[level, pl.ds(STRIDE, TR, stride=STRIDE), :]], 0
        )
        hi, lo = split2(rim)
        parts[pl.ds(level * 2 * TR, 2 * TR), pl.ds(0, CY)] = hi
        parts[pl.ds(level * 2 * TR, 2 * TR), pl.ds(CY, CY)] = lo
    fixed = jnp.dot(parts[pl.ds(0, LEV * 2 * TR), :], weights[:, pl.ds(CY, CY)], preferred_element_type=F32)
    for level in range(LEV):
        at = level * 2 * TR
        def beside(row):
            return ue[level, pl.ds(row, TR, stride=STRIDE), :]

        for row, add in (
            (0, fixed[at : at + TR] + beside(6)),
            (1, beside(7)),
            (CX - 2, beside(STRIDE)),
            (CX - 1, fixed[at + TR : at + 2 * TR] + beside(STRIDE + 1)),
        ):
            place = pl.ds(row, TR, stride=CX)
            ua[level, place, :] = ua[level, place, :] - 0.025 * add

    for copy in rows + edges + kvrows + kvedges:
        copy.wait_send()
    pltpu.make_async_copy(req.at[pl.ds(0, DEV - 1)], req.at[pl.ds(0, DEV - 1)], req_s).wait()
    pltpu.make_async_copy(rep.at[pl.ds(0, DEV - 1)], rep.at[pl.ds(0, DEV - 1)], rep_s).wait()


def smooth_kernel(us, ua, out, held, side_weights, side_out, sem):
    row, col = iota((CY, CY), 0), iota((CY, CY), 1)
    goal = (row % 32) // 16 * 2 + row % 2
    for t in range(TR):
        hit = (row < 64) & ((row % 16) // 2 == t) & (col == (goal + CY - 2) % CY)
        side_weights[:, pl.ds(t * CY, CY)] = jnp.where(hit, 1.0, 0.0).astype(BF16)

    def sides(start, levels):
        height = levels * CX

        def cells(first):
            return us[pl.ds(start, levels), pl.ds(first, CX), :].reshape(height, CY)

        lane = iota((height, CY), 1)
        u = cells(8)
        q = 2.0 * (cells(7) + cells(9)) - 8.0 * u
        across = jnp.where(
            lane < 16,
            jnp.where(lane % 2 == 1, pltpu.roll(q, 1, 1), 0.0),
            jnp.where(lane % 2 == 0, pltpu.roll(q, CY - 1, 1), 0.0),
        )
        side = u + across
        rest = side - side.astype(BF16).astype(F32)
        both = jnp.where(lane < 32, side, jnp.where(lane < 64, pltpu.roll(rest, 32, 1), 0.0))
        side_out[pl.ds(start * CX, height), :] = jnp.dot(
            both.astype(BF16), side_weights[...], preferred_element_type=F32
        )

    copies = []
    first = 0
    for block, count in enumerate((12, 12, 12, 12, 12, 6, 4, 2)):
        if block == 0:
            sides(0, count)
        if block == 1:
            sides(count, LEV - count)
        for level in range(first, first + count):
            for t in range(TR):
                edge = side_out[pl.ds(level * CX, CX), pl.ds(t * CY, CY)]
                held[t, level] = ua[level, pl.ds(t * CX, CX), :] - 0.025 * edge
        levels = pl.ds(first, count)
        first += count
        copy = pltpu.make_async_copy(held.at[:, levels], out.at[:, levels], sem.at[block])
        copy.start()
        copies.append(copy)
    for copy in copies:
        copy.wait()


def local(tracers, group_dest, group_slot, diffusivity, surface_flux):
    any_spec = pl.BlockSpec(memory_space=pltpu.HBM)
    dma = pltpu.SemaphoreType.DMA
    us, ua = pl.pallas_call(
        exchange_kernel,
        out_shape=(
            pltpu.VMEM((LEV, 32, CY), F32),
            pltpu.VMEM((LEV, TR * CX, CY), F32),
        ),
        in_specs=[any_spec] * 5,
        out_specs=(pl.BlockSpec(memory_space=pltpu.VMEM),) * 2,
        scratch_shapes=[
            pltpu.VMEM((LEV, UROWS, CY), F32),
            pltpu.VMEM((LEV, UROWS, CY), F32),
            pltpu.VMEM((TR, LEV, CX, CY), F32),
            pltpu.VMEM((CX, CY), jnp.int32),
            pltpu.VMEM((CX, CY), jnp.int32),
            pltpu.VMEM((VALS, SLOTS), F32),
            pltpu.VMEM((SLOTS, 256), BF16),
            pltpu.VMEM((CAP * DEV, SLOTS), BF16),
            pltpu.VMEM((SLOTS, 256), BF16),
            pltpu.VMEM((CX, CY), F32),
            pltpu.VMEM((DEV, SLOTS), BF16),
            pltpu.VMEM((16, SLOTS), BF16),
            pltpu.VMEM((CAP * DEV, SLOTS), BF16),
            pltpu.VMEM((DEV, 2 * CAP * CY), BF16),
            pltpu.VMEM((DEV, 1, CY), F32),
            pltpu.VMEM((DEV, 1, CY), F32),
            pltpu.VMEM((DEV, 4, CY), F32),
            pltpu.VMEM((DEV, 4, CY), F32),
            pltpu.VMEM((2 * VALS, CAP * DEV), BF16),
            pltpu.VMEM((VALS, SLOTS), F32),
            pltpu.VMEM((VALS, CX, CY), F32),
            pltpu.VMEM((3, CX, CY), F32),
            pltpu.VMEM((6, 3, CX, CY), F32),
            pltpu.VMEM((VALS, 8, CY), F32),
            pltpu.VMEM((LEV, 8 * (TR + 1), CY), F32),
            pltpu.VMEM((2, 9, CX, CY), F32),
            pltpu.VMEM((6, 9, CX, CY), F32),
            pltpu.VMEM((LEV, 24, CY), F32),
            pltpu.VMEM((LEV, 24, CY), F32),
            pltpu.VMEM((3, 24, CY), F32),
            pltpu.VMEM((LEV, CX, CY), F32),
            pltpu.VMEM((LEV, 8, CY), F32),
            pltpu.VMEM((LEV, 24, CY), F32),
            pltpu.VMEM((36 * TR * CX, 2 * CY), BF16),
            pltpu.VMEM((2 * CY, 2 * CY), BF16),
            dma((4,)), dma, dma, dma, dma, dma,
            dma((2 * TR,)), dma((2 * TR,)), dma((6,)), dma((6,)),
            dma((2,)), dma((2,)), dma((6,)), dma((6,)),
        ],
        compiler_params=pltpu.CompilerParams(
            collective_id=0, has_side_effects=True, vmem_limit_bytes=48 << 20
        ),
        name="exchange",
    )(
        *(
            pltpu.with_memory_space_constraint(x, pltpu.HBM)
            for x in (tracers, group_dest, group_slot, diffusivity, surface_flux)
        )
    )
    whole = pl.BlockSpec(memory_space=pltpu.VMEM)
    return pl.pallas_call(
        smooth_kernel,
        out_shape=jax.ShapeDtypeStruct(tracers.shape, F32),
        in_specs=[whole] * 2,
        out_specs=pl.BlockSpec(memory_space=pl.ANY),
        scratch_shapes=[
            pltpu.VMEM((TR, LEV, CX, CY), F32),
            pltpu.VMEM((CY, TR * CY), BF16),
            pltpu.VMEM((LEV * CX, TR * CY), F32),
            dma((8,)),
        ],
        compiler_params=pltpu.CompilerParams(vmem_limit_bytes=16 << 20),
        name="smooth",
    )(us, ua)


def solution(mesh):
    placed = (
        P(None, None, "fx", "fy"),
        P("fx", "fy"),
        P("fx", "fy"),
        P(None, ("fx", "fy")),
        P(None, ("fx", "fy")),
    )
    return jax.shard_map(
        local, mesh=mesh, in_specs=placed, out_specs=P(None, None, "fx", "fy"), check_vma=False
    )
```
